512 devices in a mesh: section: 4 (over x), replica: 16 (over z_lo, y), expert: 8 (over z_hi, core).
Axes of the slice: x: 4, y: 4, z: 16 (z_hi: 4, z_lo: 4; z = z_hi * 4 + z_lo), core: 2. Of those that a mesh axis runs over, the one named last changes fastest.
Arguments:
- tokens: bfloat16 [3, 256, 1536], P(None, 'replica'), may hold values from -6 to 6
- attn_gain: float32 [4, 1536], P('section'), may hold values from 0.25 to 1.75
- w_query: bfloat16 [4, 1536, 2048], P('section', None, 'expert'), may hold values from -0.15625 to 0.15625
- w_keyval: bfloat16 [4, 1536, 8, 128], P('section', None, 'expert'), may hold values from -0.15625 to 0.15625
- sinks: float32 [4, 32], P('section', 'expert'), may hold values from -2 to 260
- w_out: bfloat16 [4, 2048, 1536], P('section', 'expert'), may hold values from -0.125 to 0.125
- ffn_gain: float32 [4, 1536], P('section'), may hold values from 0.25 to 1.75
- router: bfloat16 [4, 1536, 16], P('section'), may hold values from -0.15625 to 0.15625
- w_gate_up: bfloat16 [4, 16, 2, 1536, 2048], P('section', 'replica', None, None, 'expert'), may hold values from -0.15625 to 0.15625
- w_down: bfloat16 [4, 16, 2048, 1536], P('section', 'replica', 'expert'), may hold values from -0.125 to 0.125
- kv_pool: bfloat16 [4, 2048, 16, 8, 128], P('section', 'replica', None, 'expert'), may hold values from -6 to 6
- block_table: int32 [256, 8], P('replica'), may hold values from 0 to 127, as said below
- lengths: int32 [256], P('replica'), may hold values from 1 to 128, as said below
- expert_ids: int32 [4, 3, 256, 4], P('section', None, 'replica'), may hold values from 0 to 15, all different within a row; in each aligned block of 16 rows (0 to 15, 16 to 31, ..., all dimensions but the last counted through in order) at most 5 rows name the same one
Outputs:
- layer_out: bfloat16 [4, 3, 256, 1536], P('section', None, 'replica', 'expert')
- fresh_kv: bfloat16 [4, 3, 256, 8, 128], P('section', None, 'replica', 'expert')
The draws below stay inside these ranges and needn't reach their ends.
Inputs may be any that keep to these rules, and one draw needn't show every extreme that they name: `block_table`: rows 0 to 11 of each replica are its own requests and index its own pool; its last 4 rows are requests taken over from the replica before it (replica 0 from the last one) and index that replica's pool. All blocks named in one pool are different. `lengths`: some request has exactly 128 cached tokens. `expert_ids`: A row names 4 different experts. For each layer and step, at most 5 of one replica's 16 rows name the same expert, and that count is reached.
All inputs are finite; a program needn't handle non-finite values.
Results may differ from the reference program's by a relative error of at most 0.027.
Values may be sent and summed in bfloat16 or wider, within the bound.
A program may use at most 64 MiB of HBM per device.

```python
import math
import jax
import jax.numpy as jnp
import numpy as np
from jax import lax

D = 1536
QH = 32
KVH = 8
HD = 64
FF = 2048
TOP = 4
STEPS = 3
BLK = 16
ROWS = 16
NBLK = 8
LAYERS = 4
EXPERTS = 16
MIG = 4
CTX = 128
POOL = 128
CAP = 5
N_REPLICA = 16
N_EXPERT = 8


def draw_sinks(key, part):
    key = jax.random.fold_in(key, 23)
    values = jax.random.uniform(key, (LAYERS, QH), jnp.float32, -2.0, 2.0)
    return values


def draw_lengths(key, part):
    key = jax.random.fold_in(key, 17)
    values = jax.random.randint(key, (N_REPLICA * ROWS,), 1, CTX + 1)
    spot = jax.random.randint(jax.random.fold_in(key, 1), (), 0, N_REPLICA * ROWS)
    return values.at[spot].set(CTX).astype(jnp.int32)


def draw_block_table(key, part):
    key = jax.random.fold_in(key, 11)
    replica_keys = jax.random.split(key, N_REPLICA)
    orders = jax.vmap(lambda single: jax.random.permutation(single, POOL))(replica_keys)
    own_part = orders[:, :(ROWS - MIG) * NBLK].reshape(N_REPLICA, ROWS - MIG, NBLK)
    handed = jnp.roll(orders[:, (ROWS - MIG) * NBLK:], 1, axis=0).reshape(N_REPLICA, MIG, NBLK)
    return jnp.concatenate([own_part, handed], axis=1).reshape(N_REPLICA * ROWS, NBLK).astype(jnp.int32)


def steps_of(key, dims, shards, smallest, largest):
    level, own = 1.0, jax.random.fold_in(key, 6)
    for axis_at, blocks in shards:
        draws = jnp.exp(jax.random.uniform(jax.random.fold_in(own, axis_at), (blocks,), jnp.float32, smallest / len(shards), largest / len(shards)))
        level = level * jnp.repeat(draws, dims[axis_at] // blocks).reshape([-1 if axis == axis_at else 1 for axis in range(len(dims))])
    return level


def deal_out(key, own, number, rows, count, top, most, lean):
    order = jax.random.permutation(key, count)
    crowded, ordinary = portions_of(count, rows * top, most, lean, True), portions_of(count, rows * top, most, lean, False)
    places = jnp.arange(count)

    def named(sizes, rotation):
        used = int((sizes > 0).sum())
        fixed = max(1, used // 4)
        passed = fixed + (places - fixed + rotation * (used - fixed)) % max(1, count - fixed)
        return jnp.zeros((count,), jnp.int32).at[order[jnp.where(places < fixed, places, passed)]].set(jnp.asarray(sizes, jnp.int32))

    sizes = jnp.where(number % 4 == 0, named(crowded, number // 4), named(ordinary, number - number // 4 - 1))
    mixed = jax.random.permutation(jax.random.fold_in(own, 3), count)
    giver, receiver = mixed[0:count // 2 * 2:2], mixed[1:count // 2 * 2:2]
    margin = jnp.minimum(sizes[giver] - 1, most - sizes[receiver]) // 2
    margin = jnp.where((giver == order[0]) | (receiver == order[0]) | (sizes[receiver] == 0), 0, jnp.maximum(margin, 0))
    passed = jax.random.randint(jax.random.fold_in(own, 4), (count // 2,), 0, 1 << 20) % (margin + 1)
    sizes = sizes.at[giver].add(-passed).at[receiver].add(passed)
    items = jnp.searchsorted(jnp.cumsum(sizes), jnp.arange(rows * top), side="right").astype(jnp.int32)
    listing = items.reshape(top, rows).T
    listing = listing[jax.random.permutation(jax.random.fold_in(own, 1), rows)]
    rotation = jax.random.randint(jax.random.fold_in(own, 2), (rows, 1), 0, top)
    return jnp.take_along_axis(listing, (jnp.arange(top)[None, :] + rotation) % top, axis=1)


def portions_of(amount, total, limit, lean, full):
    portions = [(1 << 20) // math.isqrt(standing ** lean) + 1 for standing in range(1, amount + 1)]
    largest = limit if full else min(limit, max(-(-total // amount), total * portions[0] // sum(portions)))
    least = 1 if total - largest >= amount - 1 else 0
    holding, rest = [largest] + [least] * (amount - 1), total - largest - least * (amount - 1)
    while rest > 0:
        movable = [i for i in range(1, amount) if holding[i] < largest] or [i for i in range(1, amount) if holding[i] < limit]
        pool, left = sum([portions[i] for i in movable]), rest
        for i in movable:
            addition = min(limit - holding[i], max(1, left * portions[i] // pool), rest)
            holding[i] = holding[i] + addition
            rest = rest - addition
    return np.array(holding)


def normal_values(stream_key, extent, spread, bound, cuts=(), kind=jnp.bfloat16):
    entries = spread * jax.random.normal(stream_key, extent, jnp.float32)
    if cuts:
        entries = entries * steps_of(stream_key, extent, cuts, -0.22, 0.18)
    return jnp.clip(entries, -bound, bound).astype(kind)


def setup_inputs(seed: int = 0) -> dict:
    splits = jax.random.split(jax.random.key(seed), 15)
    tokens = normal_values(splits[0], (STEPS, N_REPLICA * ROWS, D), 1.0, 6.0, ((1, 16),))
    attn_gain = jnp.clip(1.0 + 0.15 * jax.random.normal(splits[1], (LAYERS, D), jnp.float32), 0.25, 1.75)
    w_query = normal_values(splits[2], (LAYERS, D, QH * HD), D ** -0.5, 0.15625, ((0, 4), (2, 8)))
    w_keyval = normal_values(splits[3], (LAYERS, D, KVH, 2 * HD), D ** -0.5, 0.15625, ((0, 4), (2, 8)))
    sinks = draw_sinks(jax.random.fold_in(splits[14], 71), 0)
    w_out = normal_values(splits[5], (LAYERS, QH * HD, D), (QH * HD) ** -0.5, 0.125, ((0, 4), (1, 8)))
    ffn_gain = jnp.clip(1.0 + 0.15 * jax.random.normal(splits[6], (LAYERS, D), jnp.float32), 0.25, 1.75)
    router = normal_values(splits[7], (LAYERS, D, EXPERTS), D ** -0.5, 0.15625, ((0, 4),))
    w_gate_up = normal_values(splits[8], (LAYERS, EXPERTS, 2, D, FF), D ** -0.5, 0.15625, ((0, 4), (1, 16), (4, 8)))
    w_down = normal_values(splits[9], (LAYERS, EXPERTS, FF, D), FF ** -0.5, 0.125, ((0, 4), (1, 16), (2, 8)))
    kv_pool = normal_values(splits[10], (LAYERS, N_REPLICA * POOL, BLK, KVH, 2 * HD), 1.0, 6.0, ((0, 4), (1, 16), (3, 8)))
    block_table = draw_block_table(jax.random.fold_in(splits[14], 71), 0)
    lengths = draw_lengths(jax.random.fold_in(splits[14], 71), 0)
    expert_ids_keys = jax.random.split(jax.random.fold_in(splits[13], 1), LAYERS * STEPS * (N_REPLICA * ROWS) // ROWS)
    expert_ids_turns = jax.random.permutation(jax.random.fold_in(splits[13], 3), LAYERS * STEPS * (N_REPLICA * ROWS) // ROWS)
    expert_ids = jax.vmap(lambda own, number: deal_out(jax.random.fold_in(splits[13], 2), own, number, ROWS, EXPERTS, TOP, CAP, 2))(expert_ids_keys, expert_ids_turns).reshape((LAYERS, STEPS, N_REPLICA * ROWS, TOP))
    return {"tokens": tokens, "attn_gain": attn_gain, "w_query": w_query, "w_keyval": w_keyval, "sinks": sinks, "w_out": w_out, "ffn_gain": ffn_gain, "router": router, "w_gate_up": w_gate_up, "w_down": w_down, "kv_pool": kv_pool, "block_table": block_table, "lengths": lengths, "expert_ids": expert_ids}


EPS = 1e-05
THETA = 150000.0
NEG = -1e+30

def normed(values, gain):
    wide = values.astype(jnp.float32)
    mean_sq = lax.optimization_barrier(jnp.mean(wide * wide, axis=-1, keepdims=True))
    return (wide * lax.rsqrt(mean_sq + EPS) * gain).astype(jnp.bfloat16)

def rotated(vectors, places):
    half = vectors.shape[-1] // 2
    freq = THETA ** (-2.0 * jnp.arange(half).astype(jnp.float32) / vectors.shape[-1])
    angle = places.astype(jnp.float32)[:, None] * freq[None, :]
    cosine = jnp.cos(angle)[:, None, :]
    sine = jnp.sin(angle)[:, None, :]
    first = vectors[..., :half]
    second = vectors[..., half:]
    return jnp.concatenate([first * cosine - second * sine, second * cosine + first * sine], axis=-1)

def attend(query, cache, live_len, fresh, step_at, sink):
    head_dim = query.shape[-1]
    scale = head_dim ** (-0.5)
    query_f = query.astype(jnp.float32)
    past_keys = cache[..., :head_dim].astype(jnp.float32)
    past_vals = cache[..., head_dim:].astype(jnp.float32)
    score = jnp.einsum('rkgd,rckd->rkgc', query_f, past_keys) * scale
    live = jnp.arange(cache.shape[1])[None, :] < live_len[:, None]
    score = jnp.where(live[:, None, None, :], score, NEG)
    new_keys = fresh[..., :head_dim].astype(jnp.float32)
    new_vals = fresh[..., head_dim:].astype(jnp.float32)
    recent = jnp.einsum('rkgd,srkd->rkgs', query_f, new_keys) * scale
    seen = jnp.arange(fresh.shape[0]) <= step_at
    recent = jnp.where(seen[None, None, None, :], recent, NEG)
    peak = jnp.maximum(jnp.maximum(lax.optimization_barrier(jnp.max(score, -1)), lax.optimization_barrier(jnp.max(recent, -1))), sink[None])
    past_w = jnp.exp(score - peak[..., None])
    new_w = jnp.exp(recent - peak[..., None])
    total = lax.optimization_barrier(jnp.sum(past_w, -1)) + lax.optimization_barrier(jnp.sum(new_w, -1)) + jnp.exp(sink[None] - peak)
    past_b = (past_w / total[..., None]).astype(jnp.bfloat16).astype(jnp.float32)
    new_b = (new_w / total[..., None]).astype(jnp.bfloat16).astype(jnp.float32)
    merged = jnp.einsum('rkgc,rckd->rkgd', past_b, past_vals) + jnp.einsum('rkgs,srkd->rkgd', new_b, new_vals)
    return merged.astype(jnp.bfloat16)

def expert_terms(mlp_in, chosen, share, gate_up, down, room):
    row_total = mlp_in.shape[0]

    def add_expert(expert_index, running):
        hit = jnp.any(chosen == expert_index, axis=-1)
        order = jnp.argsort(jnp.where(hit, 0, 1).astype(jnp.int32), stable=True)[:room]
        picked = mlp_in[order]
        gate_part = jnp.dot(picked, gate_up[expert_index, 0], preferred_element_type=jnp.float32)
        up_part = jnp.dot(picked, gate_up[expert_index, 1], preferred_element_type=jnp.float32)
        hidden = (jax.nn.silu(gate_part) * up_part).astype(jnp.bfloat16)
        hidden_f = hidden.astype(jnp.float32).reshape(room, N_EXPERT, -1)
        down_f = down[expert_index].astype(jnp.float32).reshape(N_EXPERT, -1, mlp_in.shape[1])
        pieces = jnp.einsum('cjf,jfd->jcd', hidden_f, down_f)
        pieces = lax.optimization_barrier(pieces.astype(jnp.bfloat16)).astype(jnp.float32)
        output = lax.optimization_barrier(lax.optimization_barrier(jnp.sum(pieces, 0)).astype(jnp.bfloat16)).astype(jnp.float32)
        weight = share[order, expert_index]
        return running.at[order].add(weight[:, None] * output)
    start = jnp.zeros((row_total, mlp_in.shape[1]), jnp.float32)
    return lax.fori_loop(0, EXPERTS, add_expert, start)

def reference(tokens, attn_gain, w_query, w_keyval, sinks, w_out, ffn_gain, router, w_gate_up, w_down, kv_pool, block_table, lengths, expert_ids):
    row_total = N_REPLICA * ROWS
    row_ids = jnp.arange(row_total).astype(jnp.int32)
    owner = row_ids // ROWS
    taken = row_ids % ROWS >= ROWS - MIG
    source = jnp.where(taken, (owner + N_REPLICA - 1) % N_REPLICA, owner).astype(jnp.int32)
    global_blocks = (source[:, None] * POOL + block_table).astype(jnp.int32)
    group = QH // KVH
    caches = [kv_pool[layer][global_blocks].reshape(row_total, CTX, KVH, 2 * HD) for layer in range(LAYERS)]
    fresh = [jnp.zeros((STEPS, row_total, KVH, 2 * HD), jnp.bfloat16) for layer in range(LAYERS)]
    outputs = [[None] * STEPS for layer in range(LAYERS)]
    expert_range = jnp.arange(EXPERTS).astype(jnp.int32)
    for step_at in range(STEPS):
        current = tokens[step_at]
        places = lengths + step_at
        for layer in range(LAYERS):
            normal_in = normed(current, attn_gain[layer])
            query = jnp.dot(normal_in, w_query[layer], preferred_element_type=jnp.float32).reshape(row_total, QH, HD)
            query = rotated(query, places).astype(jnp.bfloat16).reshape(row_total, KVH, group, HD)
            keyval = jnp.dot(normal_in, w_keyval[layer].reshape(D, KVH * 2 * HD), preferred_element_type=jnp.float32).reshape(row_total, KVH, 2 * HD)
            new_entry = jnp.concatenate([rotated(keyval[..., :HD], places), keyval[..., HD:]], axis=-1).astype(jnp.bfloat16)
            fresh[layer] = fresh[layer].at[step_at].set(new_entry)
            attended = attend(query, caches[layer], lengths, fresh[layer], step_at, sinks[layer].reshape(KVH, group))
            mixed = jnp.dot(attended.reshape(row_total, QH * HD), w_out[layer], preferred_element_type=jnp.float32)
            after_attn = (current.astype(jnp.float32) + mixed).astype(jnp.bfloat16)
            mlp_in = normed(after_attn, ffn_gain[layer])
            logits = jnp.dot(mlp_in, router[layer], preferred_element_type=jnp.float32)
            chosen = expert_ids[layer, step_at]
            chosen_hot = (chosen[:, :, None] == expert_range[None, None, :]).astype(jnp.float32)
            gates = jax.nn.sigmoid(lax.optimization_barrier(jnp.sum(chosen_hot * logits[:, None, :], -1)))
            weight = gates / lax.optimization_barrier(jnp.sum(gates, -1, keepdims=True))
            share = lax.optimization_barrier(jnp.sum(chosen_hot * weight[..., None], 1))
            moe = expert_terms(mlp_in, chosen, share, w_gate_up[layer], w_down[layer], N_REPLICA * CAP)
            current = (after_attn.astype(jnp.float32) + moe).astype(jnp.bfloat16)
            outputs[layer][step_at] = current
    layer_out = jnp.stack([jnp.stack(outputs[layer], 0) for layer in range(LAYERS)], 0)
    fresh_kv = jnp.stack(fresh, 0)
    return (layer_out, fresh_kv)
```

```python
import math

import jax
import jax.numpy as jnp
from jax import lax
from jax.experimental import pallas as pl
from jax.experimental.pallas import tpu as pltpu
from jax.sharding import PartitionSpec as P

MESH = pl.DeviceIdType.MESH
F32 = jnp.float32
BF16 = jnp.bfloat16
EPS = 1e-05
THETA = 150000.0
NEG = -1e30
T = 3
R = 16
D = 1536
H = 768
CW = 256
NR = 16
NZ = 4
SLOT = 5
MIG = 4
NB = 8
NS = 4

ORDER = (
    ("I", 0), ("A", 0), ("B", 0), ("I", 1), ("A", 1), ("I", 2), ("B", 1), ("A", 2),
    ("C", 0), ("B", 2), ("D", 0), ("C", 1), ("E", 0), ("F", 0), ("C", 2), ("G", 0),
    ("E", 1), ("D", 1), ("F", 1), ("E", 2), ("G", 1), ("D", 2), ("H", 0), ("F", 2),
    ("G", 2), ("S", 0), ("S", 1), ("H", 1), ("S", 2), ("H", 2),
)


def iota(shape, axis):
    return lax.broadcasted_iota(jnp.int32, shape, axis).astype(F32)


def div(value, by):
    return jnp.floor((value + 0.5) * (1.0 / by))


def mod(value, by):
    return value - by * div(value, by)


def dot(a, b):
    return jnp.dot(a, b, preferred_element_type=F32)


def dot_t(a, b):
    return lax.dot_general(a, b, (((1,), (1,)), ((), ())), preferred_element_type=F32)


def one_hot(cond):
    return jnp.where(cond, 1.0, 0.0).astype(BF16)


def kernel(
    tok, again, wq, wkv, sinks, wout, fgain, router, wgu, wdown, pool, table_v, table_s, lens, ids,
    out, fresh_out,
    wqkv_v, wout_v, wgu_v, wdown_v, pool_v, cache, leave, next_v, next_s,
    xb, xf, q4, fresh, rope_c, rope_s, bias,
    fold, rep, sel, pack, place, mask_t, comb,
    apo, asend, arecv, ar, h1, hx, disp, recv, yo, ysend, yrecv, rsend, rrecv, psend, xin, bsend, brecv, qp, fin,
    wsem, tsem, msem, ssend, srecv,
):
    s = lax.axis_index("section")
    r = lax.axis_index("replica")
    e = lax.axis_index("expert")
    c = lax.rem(e, 2)
    zh = lax.div(e, 2)
    oc = 1 - c
    sib = {"expert": e + 1 - 2 * c}
    after = lax.rem(s + 1, NS)
    before = lax.rem(s + NS - 1, NS)
    r_next = lax.rem(r + 1, NR)
    r_prev = lax.rem(r + NR - 1, NR)
    z_peers = [{"expert": lax.rem(e + 2 * k, 2 * NZ)} for k in range(1, NZ)]
    r_peers = [lax.rem(r + k, NR) for k in range(1, NR)]

    token_copies = [
        pltpu.make_async_copy(tok.at[t, :, pl.ds(h * H, H)], xb.at[t, h], tsem.at[2 * t + h])
        for t in range(T)
        for h in range(2)
    ]

    @pl.when(s == 0)
    def _():
        for copy in token_copies:
            copy.start()

    local = [(pool, pool_v)]
    for h in range(2):
        rows = pl.ds(h * H, H)
        local.append((wq.at[rows], wqkv_v.at[h, :, pl.ds(0, 256)]))
        local.append((wkv.at[rows], wqkv_v.at[h, :, pl.ds(256, 128)]))
    for h in range(2):
        local.append((wout.at[:, pl.ds(h * H, H)], wout_v.at[h]))
    for h in range(2):
        for k in range(2):
            local.append((wgu.at[k, pl.ds(h * H, H)], wgu_v.at[h, :, pl.ds(k * 256, 256)]))
    for h in range(2):
        local.append((wdown.at[:, pl.ds(h * H, H)], wdown_v.at[h]))
    local = [pltpu.make_async_copy(a, b, wsem.at[i]) for i, (a, b) in enumerate(local)]
    for copy in local:
        copy.start()

    barrier = pltpu.get_barrier_semaphore()
    greeted = [sib, *z_peers, *[{"replica": p} for p in r_peers]]
    for k in range(NZ):
        lane = lax.rem(e + 2 * k, 2 * NZ)
        greeted += [{"section": after, "expert": lane}, {"section": before, "expert": lane}]
    for peer in greeted:
        pl.semaphore_signal(barrier, inc=1, device_id=peer, device_id_type=MESH)

    row16 = iota((R, 1), 0)
    length = jnp.zeros((R, 1), F32)
    for i in range(R):
        length = jnp.where(row16 == i, lens[i].astype(F32), length)
    lane = iota((1, 128), 1)
    freq = jnp.exp(mod(lane, 32) * (-2.0 / 64 * math.log(THETA)))
    sign = jnp.where(mod(lane, 64) < 32, -1.0, 1.0)
    for t in range(T):
        angle = (length + float(t)) * freq
        rope_c[t] = jnp.cos(angle)
        rope_s[t] = jnp.sin(angle) * sign
    inside = iota((R, R * 128), 1) - iota((R, R * 128), 0) * 128.0
    bias[...] = jnp.where((inside >= 0) & (inside < length), 0.0, NEG)
    a, b = iota((256, 128), 0), iota((256, 128), 1)
    fold[...] = jnp.where(mod(a, 64) == b, 0.125, 0.0).astype(BF16)
    a, b = iota((128, 256), 0), iota((128, 256), 1)
    rep[...] = one_hot(a - 64 == mod(b, 64))

    def packed_at(q):
        block = div(q, R * SLOT)
        rest = q - block * (R * SLOT)
        source = div(rest, SLOT)
        return source * 16 + block * SLOT + rest - source * SLOT

    sel[...] = one_hot(packed_at(iota((240, 1), 0)) == iota((240, 256), 1))
    pack[...] = one_hot(packed_at(iota((1, 240), 1)) == iota((256, 240), 0))
    spread = one_hot(div(iota((256, NR), 0), 16) == iota((256, NR), 1))
    spread_t = one_hot(div(iota((NR, 256), 1), 16) == iota((NR, 256), 0))
    tile = one_hot(mod(iota((R, 48), 1), 16) == iota((R, 48), 0))
    tile_t = one_hot(mod(iota((48, R), 0), 16) == iota((48, R), 1))
    earlier = one_hot(iota((R, R), 0) < iota((R, R), 1))
    at = mod(iota((256, 48), 0), 16)
    block = div(at, SLOT)
    wants = jnp.where(block == div(iota((256, 48), 1), 16), at - block * SLOT + 1.0, -1.0)
    at_t = mod(iota((48, 256), 1), 16)
    block_t = div(at_t, SLOT)
    wants_t = jnp.where(block_t == div(iota((48, 256), 0), 16), at_t - block_t * SLOT + 1.0, -1.0)
    chosen_rows = []
    for t in range(T):
        named = ids[t].astype(F32)
        hot = jnp.zeros((NR, R), F32)
        for k in range(4):
            hot = jnp.where(named[k : k + 1, :] == iota((NR, R), 0), 1.0, hot)
        code = (hot * (dot(hot.astype(BF16), earlier) + 1.0)).astype(BF16)
        place[t] = one_hot(dot(spread, dot(code, tile).astype(BF16)) == wants)
        code_t = dot_t(tile_t, code)
        mask_t[t] = jnp.where(dot(code_t.astype(BF16), spread_t) == wants_t, 1.0, 0.0)
        chosen_rows.append(jnp.where(code_t[:R] > 0, 1.0, 0.0))

    local[0].wait()
    for i in range((R - MIG) * NB):
        cache[i] = pool_v[table_s[i % NB, i // NB]]
    pl.semaphore_wait(barrier, len(greeted))

    def remote(src, dst, index, device):
        return pltpu.make_async_remote_copy(
            src_ref=src, dst_ref=dst, send_sem=ssend.at[index], recv_sem=srecv.at[index],
            device_id=device, device_id_type=MESH,
        )

    table_copy = remote(table_v, next_v, 0, {"replica": r_prev})
    table_copy.start()

    def gain_half(gain, h):
        return jnp.where(h == 0, gain[:, :H], gain[:, H:])

    def attn_half(t, h):
        x = xb[t, h].astype(F32) * gain_half(again, h)
        return dot(x.astype(BF16), wqkv_v[h])

    def attn_in(t):
        x = jnp.concatenate([xb[t, 0], xb[t, 1]], axis=1).astype(F32)
        scale = lax.rsqrt(jnp.mean(x * x, axis=-1, keepdims=True) + EPS)
        qkv = (qp[t] + attn_half(t, oc)) * scale
        cosine, sine = rope_c[t], rope_s[t]

        def turned(v):
            width = v.shape[1]
            low = mod(iota((R, width), 1), 64) < 32
            return jnp.where(low, pltpu.roll(v, width - 32, 1), pltpu.roll(v, 32, 1))

        q = qkv[:, :256]
        q = q * jnp.concatenate([cosine, cosine], 1) + turned(q) * jnp.concatenate([sine, sine], 1)
        kv = qkv[:, 256:]
        keys = iota((R, 128), 1) < 64
        kv = kv * jnp.where(keys, cosine, 1.0) + jnp.where(keys, turned(kv) * sine, 0.0)
        fresh[pl.ds(t * R, R)] = kv.astype(BF16)
        fresh_out[t] = kv.astype(BF16)
        q = jnp.concatenate([q] * 4, axis=0)
        head = div(iota((64, 256), 1), 64) == div(iota((64, 256), 0), 16)
        q4[t] = dot(jnp.where(head, q, 0.0).astype(BF16), fold[...]).astype(BF16)

    def attend(t):
        q = q4[t]
        past = cache[...].reshape(R * 128, 128)
        new = fresh[pl.ds(0, R * (t + 1))]
        score = dot_t(q, past)
        score = jnp.concatenate([score[g * R : g * R + R] + bias[...] for g in range(4)], axis=0)
        recent = dot_t(q, new)
        width = R * (t + 1)
        same = mod(iota((64, width), 1), 16) == mod(iota((64, width), 0), 16)
        recent = jnp.where(same, recent, NEG)
        group = div(iota((64, 1), 0), 16)
        sink = jnp.zeros((64, 1), F32)
        for g in range(4):
            sink = jnp.where(group == g, sinks[0, g], sink)
        peak = jnp.maximum(jnp.max(score, -1, keepdims=True), jnp.max(recent, -1, keepdims=True))
        peak = jnp.maximum(peak, sink)
        past_w = jnp.exp(score - peak)
        new_w = jnp.exp(recent - peak)
        total = jnp.sum(past_w, -1, keepdims=True) + jnp.sum(new_w, -1, keepdims=True)
        share = 1.0 / (total + jnp.exp(sink - peak))
        merged = dot((past_w * share).astype(BF16), past) + dot((new_w * share).astype(BF16), new)
        wide = dot(merged.astype(BF16), rep[...])
        head = div(iota((64, 256), 1), 64) == div(iota((64, 256), 0), 16)
        wide = jnp.where(head, wide, 0.0)
        wide = wide[:R] + wide[R : 2 * R] + wide[2 * R : 3 * R] + wide[3 * R :]
        wide = wide.astype(BF16)
        asend[t] = dot(wide, wout_v[oc]).astype(BF16)
        remote(asend.at[t], arecv.at[t], 10 + t, sib).start()
        apo[t] = dot(wide, wout_v[c])

    def pair_sum(t):
        remote(asend.at[t], arecv.at[t], 10 + t, sib).wait_recv()
        ar[t, zh] = (apo[t] + arecv[t].astype(F32)).astype(BF16)
        for peer in z_peers:
            remote(ar.at[t, zh], ar.at[t, zh], 13 + t, peer).start()

    def wait_blocks(ref, sem):
        pltpu.make_async_copy(ref, ref, sem).wait()

    def all_sum(t):
        wait_blocks(ar.at[t, pl.ds(0, NZ - 1)], srecv.at[13 + t])
        total = xb[t, c].astype(F32) + (
            ar[t, 0].astype(F32) + ar[t, 1].astype(F32) + (ar[t, 2].astype(F32) + ar[t, 3].astype(F32))
        )
        half = total.astype(BF16)
        h1[t, c] = half
        remote(h1.at[t, c], h1.at[t, c], 16 + t, sib).start()
        stack = jnp.concatenate([half[:, i * CW : i * CW + CW] for i in range(3)], axis=0)
        disp[t] = dot(place[t], stack).astype(BF16).reshape(NR, 16, CW)
        for peer in r_peers:
            remote(disp.at[t, peer], recv.at[t, c, r], 22 + t, {"replica": peer}).start()
        recv[t, c, r] = disp[t, r]

        @pl.when(s < NS - 1)
        def _():
            remote(h1.at[t, c], hx.at[t], 19 + t, {"section": after}).start()

    def shares(t):
        remote(h1.at[t, c], h1.at[t, c], 16 + t, sib).wait_recv()
        x = jnp.concatenate([h1[t, 0], h1[t, 1]], axis=1).astype(F32)
        scale = lax.rsqrt(jnp.mean(x * x, axis=-1, keepdims=True) + EPS)
        normal = (x * scale * fgain[...]).astype(BF16)
        gates = chosen_rows[t] / (1.0 + jnp.exp(-dot_t(normal, router[...])))
        share = gates / jnp.sum(gates, -1, keepdims=True)
        share = jnp.concatenate([share] * 3, axis=0)
        high = share.astype(BF16)
        low = (share - high.astype(F32)).astype(BF16)
        comb[t, 0] = (dot(high, spread_t) * mask_t[t]).astype(BF16)
        comb[t, 1] = (dot(low, spread_t) * mask_t[t]).astype(BF16)

    def relay(t):
        wait_blocks(recv.at[t, 0, pl.ds(0, NR - 1)], srecv.at[22 + t])
        remote(recv.at[t, c], recv.at[t, c], 25 + t, sib).start()

    def expert(t):
        def half(h):
            rows = dot(sel[...], recv[t, h].reshape(256, CW))
            rows = jnp.concatenate([rows[i * 80 : i * 80 + 80] for i in range(3)], axis=1)
            square = jnp.sum(rows * rows, axis=-1, keepdims=True)
            return square, dot((rows * gain_half(fgain, h)).astype(BF16), wgu_v[h])

        square, both = half(c)
        remote(recv.at[t, c], recv.at[t, c], 25 + t, sib).wait_recv()
        square_o, both_o = half(oc)
        both = (both + both_o) * lax.rsqrt((square + square_o) * (1.0 / D) + EPS)
        gate, up = both[:, :256], both[:, 256:]
        hidden = (gate / (1.0 + jnp.exp(-gate)) * up).astype(BF16)
        ysend[t] = dot(hidden, wdown_v[oc]).astype(BF16)
        remote(ysend.at[t], yrecv.at[t], 28 + t, sib).start()
        yo[t] = dot(hidden, wdown_v[c])

    def give_back(t):
        remote(ysend.at[t], yrecv.at[t], 28 + t, sib).wait_recv()
        y = (yo[t] + yrecv[t].astype(F32)).astype(BF16)
        stack = jnp.concatenate([y[:, i * CW : i * CW + CW] for i in range(3)], axis=0)
        rsend[t] = dot(pack[...], stack).astype(BF16).reshape(NR, 16, CW)
        for peer in r_peers:
            remote(rsend.at[t, peer], rrecv.at[t, r], 31 + t, {"replica": peer}).start()
        rrecv[t, r] = rsend[t, r]

    def combine(t):
        wait_blocks(rrecv.at[t, pl.ds(0, NR - 1)], srecv.at[31 + t])
        rows = rrecv[t].reshape(256, CW)
        got = dot(comb[t, 0], rows) + dot(comb[t, 1], rows)
        psend[t] = jnp.concatenate([got[i * R : i * R + R] for i in range(3)], axis=1).astype(BF16)

        @pl.when(s < NS - 1)
        def _():
            for k in range(NZ):
                peer = {"section": after, "expert": lax.rem(e + 2 * k, 2 * NZ)}
                remote(psend.at[t], xin.at[t, zh], 34 + t, peer).start()

        @pl.when(s == NS - 1)
        def _():
            for peer in z_peers:
                remote(psend.at[t], fin.at[t, zh], 43 + t, peer).start()
            fin[t, zh] = psend[t]

    def total_of(first, parts):
        a, b, c_, d = (parts[k].astype(F32) for k in range(NZ))
        return (first.astype(F32) + (a + b + (c_ + d))).astype(BF16)

    def sum_in(t):
        wait_blocks(xin.at[t], srecv.at[34 + t])
        remote(h1.at[t, c], hx.at[t], 19 + t, {"section": after}).wait_recv()
        xb[t, c] = total_of(hx[t], xin.at[t])
        remote(xb.at[t, c], xb.at[t, c], 37 + t, sib).start()
        qp[t] = attn_half(t, c)

    def lane_columns(t, of):
        x = jnp.concatenate([of[t, 0], of[t, 1]], axis=1).astype(F32)
        quarter = jnp.zeros((R, 384), F32)
        for k in range(NZ):
            quarter = jnp.where(zh == k, x[:, k * 384 : k * 384 + 384], quarter)
        return jnp.where(c == 0, quarter[:, :192], quarter[:, 192:])

    def send_result(t):
        own = lane_columns(t, xb)
        bsend[t] = jnp.concatenate([own, jnp.zeros((R, 64), F32)], axis=1).astype(BF16)
        remote(bsend.at[t], brecv.at[t], 40 + t, {"section": before}).start()

    for copy in local[1:5]:
        copy.wait()

    @pl.when(s == 0)
    def _():
        for t in range(T):
            token_copies[2 * t].wait()
            token_copies[2 * t + 1].wait()
            qp[t] = attn_half(t, c)
            attn_in(t)

    table_copy.wait_recv()
    to_smem = pltpu.make_async_copy(next_v, next_s, msem)
    to_smem.start()
    to_smem.wait()
    for i in range(MIG * NB):
        leave[i] = pool_v[next_s[i % NB, R - MIG + i // NB]]
    start = (R - MIG) * NB
    leave_copy = remote(leave, cache.at[pl.ds(start, MIG * NB)], 1, {"replica": r_next})
    leave_copy.start()
    leave_copy.wait_recv()
    for copy in local[5:]:
        copy.wait()

    def on_arrival(t):
        @pl.when(s > 0)
        def _():
            sum_in(t)

    def attention(t):
        @pl.when(s > 0)
        def _():
            remote(xb.at[t, c], xb.at[t, c], 37 + t, sib).wait_recv()
            attn_in(t)

        attend(t)

    def result(t):
        @pl.when(s > 0)
        def _():
            send_result(t)

    steps = {
        "I": on_arrival, "A": attention, "B": pair_sum, "C": all_sum, "D": shares,
        "E": relay, "F": expert, "G": give_back, "H": combine, "S": result,
    }
    for name, t in ORDER:
        steps[name](t)

    @pl.when(s == NS - 1)
    def _():
        for t in range(T):
            wait_blocks(fin.at[t, pl.ds(0, NZ - 1)], srecv.at[43 + t])
            xf[t, c] = total_of(h1[t, c], fin.at[t])
            remote(xf.at[t, c], xf.at[t, c], 46 + t, sib).start()
        for t in range(T):
            remote(xf.at[t, c], xf.at[t, c], 46 + t, sib).wait_recv()
            out[t] = lane_columns(t, xf).astype(BF16)

    @pl.when(s < NS - 1)
    def _():
        for t in range(T):
            remote(bsend.at[t], brecv.at[t], 40 + t, {"section": before}).wait_recv()
            out[t] = brecv[t][:, :192]

    table_copy.wait_send()
    leave_copy.wait_send()

    def left(t, pairs):
        for index, ref in pairs:
            wait_blocks(ref, ssend.at[index + t])

    for t in range(T):
        left(t, (
            (10, asend.at[t]),
            (13, ar.at[t, pl.ds(0, NZ - 1)]),
            (16, h1.at[t, c]),
            (22, disp.at[t, pl.ds(0, NR - 1)]),
            (25, recv.at[t, c]),
            (28, ysend.at[t]),
            (31, rsend.at[t, pl.ds(0, NR - 1)]),
        ))

    @pl.when(s > 0)
    def _():
        for t in range(T):
            left(t, ((37, xb.at[t, c]), (40, bsend.at[t])))

    @pl.when(s < NS - 1)
    def _():
        for t in range(T):
            left(t, ((19, h1.at[t, c]), (34, xin.at[t])))

    @pl.when(s == NS - 1)
    def _():
        for t in range(T):
            left(t, ((43, fin.at[t, pl.ds(0, NZ - 1)]), (46, xf.at[t, c])))


def local_part(
    tokens, attn_gain, w_query, w_keyval, sinks, w_out, ffn_gain, router, w_gate_up, w_down,
    kv_pool, block_table, lengths, expert_ids,
):
    vmem = pl.BlockSpec(memory_space=pltpu.VMEM)
    smem = pl.BlockSpec(memory_space=pltpu.SMEM)
    hbm = pl.BlockSpec(memory_space=pltpu.HBM)
    table = block_table.T
    operands = [
        (tokens, hbm),
        (attn_gain, vmem),
        (w_query[0], hbm),
        (w_keyval.reshape(D, 128), hbm),
        (sinks, smem),
        (w_out[0], hbm),
        (ffn_gain, vmem),
        (router[0].T, vmem),
        (w_gate_up[0, 0], hbm),
        (w_down[0, 0], hbm),
        (kv_pool.reshape(128, 16, 128), hbm),
        (table, vmem),
        (table, smem),
        (lengths, smem),
        (expert_ids[0].transpose(0, 2, 1), vmem),
    ]
    V = pltpu.VMEM
    scratch = [
        V((2, H, 384), BF16), V((2, 256, H), BF16), V((2, H, 512), BF16), V((2, 256, H), BF16),
        V((128, 16, 128), BF16), V((128, 16, 128), BF16), V((MIG * NB, 16, 128), BF16),
        V((NB, R), jnp.int32), pltpu.SMEM((NB, R), jnp.int32),
        V((T, 2, R, H), BF16), V((T, 2, R, H), BF16), V((T, 64, 128), BF16), V((T * R, 128), BF16),
        V((T, R, 128), F32), V((T, R, 128), F32), V((R, R * 128), F32),
        V((256, 128), BF16), V((128, 256), BF16), V((240, 256), BF16), V((256, 240), BF16),
        V((T, 256, 48), BF16), V((T, 48, 256), F32), V((T, 2, 48, 256), BF16),
        V((T, R, H), F32), V((T, R, H), BF16), V((T, R, H), BF16), V((T, NZ, R, H), BF16),
        V((T, 2, R, H), BF16), V((T, R, H), BF16), V((T, NR, 16, CW), BF16),
        V((T, 2, NR, 16, CW), BF16), V((T, 80, H), F32), V((T, 80, H), BF16), V((T, 80, H), BF16),
        V((T, NR, 16, CW), BF16), V((T, NR, 16, CW), BF16), V((T, R, H), BF16),
        V((T, NZ, R, H), BF16), V((T, R, 256), BF16), V((T, R, 256), BF16),
        V((T, R, 384), F32), V((T, NZ, R, H), BF16),
        pltpu.SemaphoreType.DMA((13,)), pltpu.SemaphoreType.DMA((2 * T,)), pltpu.SemaphoreType.DMA,
        pltpu.SemaphoreType.DMA((49,)), pltpu.SemaphoreType.DMA((49,)),
    ]
    layer_out, fresh = pl.pallas_call(
        kernel,
        out_shape=(
            jax.ShapeDtypeStruct((T, R, 192), BF16),
            jax.ShapeDtypeStruct((T, R, 128), BF16),
        ),
        in_specs=[spec for _, spec in operands],
        out_specs=(vmem, vmem),
        scratch_shapes=scratch,
        compiler_params=pltpu.CompilerParams(
            collective_id=0, has_side_effects=True, vmem_limit_bytes=62 << 20
        ),
        name="layers",
    )(*[value for value, _ in operands])
    return layer_out[None], fresh.reshape(1, T, R, 1, 128)


def solution(mesh):
    return jax.shard_map(
        local_part,
        mesh=mesh,
        in_specs=(
            P(None, "replica", None),
            P("section", None),
            P("section", None, "expert"),
            P("section", None, "expert", None),
            P("section", "expert"),
            P("section", "expert", None),
            P("section", None),
            P("section", None, None),
            P("section", "replica", None, None, "expert"),
            P("section", "replica", "expert", None),
            P("section", "replica", None, "expert", None),
            P("replica", None),
            P("replica"),
            P("section", None, "replica", None),
        ),
        out_specs=(
            P("section", None, "replica", "expert"),
            P("section", None, "replica", "expert", None),
        ),
        check_vma=False,
    )
```

```python
import math

import jax
import jax.numpy as jnp
from jax import lax
from jax.experimental import pallas as pl
from jax.experimental.pallas import tpu as pltpu
from jax.sharding import PartitionSpec as P

MESH = pl.DeviceIdType.MESH
F32 = jnp.float32
BF16 = jnp.bfloat16
EPS = 1e-05
THETA = 150000.0
NEG = -1e30
T = 3
R = 16
D = 1536
H = 768
CW = 256
NR = 16
NZ = 4
SLOT = 5
MIG = 4
NB = 8
NS = 4

ORDER = (
    ("I", 0), ("A", 0), ("B", 0), ("I", 1), ("A", 1), ("I", 2), ("B", 1), ("A", 2),
    ("C", 0), ("B", 2), ("D", 0), ("C", 1), ("E", 0), ("F", 0), ("C", 2), ("G", 0),
    ("E", 1), ("D", 1), ("F", 1), ("E", 2), ("G", 1), ("D", 2), ("H", 0), ("F", 2),
    ("G", 2), ("S", 0), ("S", 1), ("H", 1), ("S", 2), ("H", 2),
)


def iota(shape, axis):
    return lax.broadcasted_iota(jnp.int32, shape, axis).astype(F32)


def div(value, by):
    return jnp.floor((value + 0.5) * (1.0 / by))


def mod(value, by):
    return value - by * div(value, by)


def dot(a, b):
    return jnp.dot(a, b, preferred_element_type=F32)


def dot_t(a, b):
    return lax.dot_general(a, b, (((1,), (1,)), ((), ())), preferred_element_type=F32)


def one_hot(cond):
    return jnp.where(cond, 1.0, 0.0).astype(BF16)


def kernel(
    tok, again, wq, wkv, sinks, wout, fgain, router, wgu, wdown, pool, table_s, lens, ids,
    out, fresh_out,
    wqkv_v, wout_v, wgu_v, wdown_v, pool_v, cache, leave, came, index_v, index_s,
    xb, xf, q4, fresh, rope_c, rope_s, bias,
    fold, rep, sel, pack, place, mask_t, comb,
    apo, asend, arecv, ar, h1, hx, disp, recv, yo, ysend, yrecv, rsend, rrecv, psend, xin, bsend, brecv, qp, fin,
    wsem, tsem, msem, ssend, srecv,
):
    s = lax.axis_index("section")
    r = lax.axis_index("replica")
    e = lax.axis_index("expert")
    c = lax.rem(e, 2)
    zh = lax.div(e, 2)
    oc = 1 - c
    sib = {"expert": e + 1 - 2 * c}
    after = lax.rem(s + 1, NS)
    before = lax.rem(s + NS - 1, NS)
    r_next = lax.rem(r + 1, NR)
    r_prev = lax.rem(r + NR - 1, NR)
    z_peers = [{"expert": lax.rem(e + 2 * k, 2 * NZ)} for k in (2, 1, 3)]
    r_peers = [lax.rem(r + k, NR) for k in range(1, NR)]

    low = lax.div(r, NR // NZ)

    def hops(start, end):
        way = lax.rem(end - start + NZ, NZ)
        half_way = lax.div(way, 2) * (1 - lax.rem(way, 2))
        return lax.rem(way + 1, NZ) - 1 - NZ * lax.rem(start, 2) * half_way

    def lane_at(z):
        return 2 * lax.rem(lax.div(z + NZ * NZ, NZ), NZ) + c

    here = NZ * zh + low
    lane_to = [lane_at(here + hops(low, lax.div(p, NR // NZ))) for p in r_peers]
    lane_from = [lane_at(here - hops(lax.div(p, NR // NZ), low)) for p in r_peers]
    r_targets = [(p, {"replica": p, "expert": lane}) for p, lane in zip(r_peers, lane_to)]

    token_copies = [
        pltpu.make_async_copy(tok.at[t, :, pl.ds(h * H, H)], xb.at[t, h], tsem.at[2 * t + h])
        for t in range(T)
        for h in range(2)
    ]

    @pl.when(s == 0)
    def _():
        for copy in token_copies:
            copy.start()

    local = [(pool, pool_v)]
    for h in range(2):
        rows = pl.ds(h * H, H)
        local.append((wq.at[rows], wqkv_v.at[h, :, pl.ds(0, 256)]))
        local.append((wkv.at[rows], wqkv_v.at[h, :, pl.ds(256, 128)]))
    for h in range(2):
        local.append((wout.at[:, pl.ds(h * H, H)], wout_v.at[h]))
    for h in range(2):
        for k in range(2):
            local.append((wgu.at[k, pl.ds(h * H, H)], wgu_v.at[h, :, pl.ds(k * 256, 256)]))
    for h in range(2):
        local.append((wdown.at[:, pl.ds(h * H, H)], wdown_v.at[h]))
    local = [pltpu.make_async_copy(a, b, wsem.at[i]) for i, (a, b) in enumerate(local)]
    for copy in local:
        copy.start()

    barrier = pltpu.get_barrier_semaphore()
    greeted = [sib, {"replica": r_prev}, *z_peers, *[{"replica": p, "expert": lane} for p, lane in zip(r_peers, lane_from)]]
    for k in range(NZ):
        lane = lax.rem(e + 2 * k, 2 * NZ)
        greeted += [{"section": after, "expert": lane}, {"section": before, "expert": lane}]
    for peer in greeted:
        pl.semaphore_signal(barrier, inc=1, device_id=peer, device_id_type=MESH)

    row16 = iota((R, 1), 0)
    length = jnp.zeros((R, 1), F32)
    for i in range(R):
        length = jnp.where(row16 == i, lens[i].astype(F32), length)
    lane = iota((1, 128), 1)
    freq = jnp.exp(mod(lane, 32) * (-2.0 / 64 * math.log(THETA)))
    sign = jnp.where(mod(lane, 64) < 32, -1.0, 1.0)
    for t in range(T):
        angle = (length + float(t)) * freq
        rope_c[t] = jnp.cos(angle)
        rope_s[t] = jnp.sin(angle) * sign
    inside = iota((R, R * 128), 1) - iota((R, R * 128), 0) * 128.0
    bias[...] = jnp.where((inside >= 0) & (inside < length), 0.0, NEG)
    a, b = iota((256, 128), 0), iota((256, 128), 1)
    fold[...] = jnp.where(mod(a, 64) == b, 0.125, 0.0).astype(BF16)
    a, b = iota((128, 256), 0), iota((128, 256), 1)
    rep[...] = one_hot(a - 64 == mod(b, 64))

    def packed_at(q):
        block = div(q, R * SLOT)
        rest = q - block * (R * SLOT)
        source = div(rest, SLOT)
        return source * 16 + block * SLOT + rest - source * SLOT

    sel[...] = one_hot(packed_at(iota((240, 1), 0)) == iota((240, 256), 1))
    pack[...] = one_hot(packed_at(iota((1, 240), 1)) == iota((256, 240), 0))
    spread = one_hot(div(iota((256, NR), 0), 16) == iota((256, NR), 1))
    spread_t = one_hot(div(iota((NR, 256), 1), 16) == iota((NR, 256), 0))
    tile = one_hot(mod(iota((R, 48), 1), 16) == iota((R, 48), 0))
    tile_t = one_hot(mod(iota((48, R), 0), 16) == iota((48, R), 1))
    earlier = one_hot(iota((R, R), 0) < iota((R, R), 1))
    at = mod(iota((256, 48), 0), 16)
    block = div(at, SLOT)
    wants = jnp.where(block == div(iota((256, 48), 1), 16), at - block * SLOT + 1.0, -1.0)
    at_t = mod(iota((48, 256), 1), 16)
    block_t = div(at_t, SLOT)
    wants_t = jnp.where(block_t == div(iota((48, 256), 0), 16), at_t - block_t * SLOT + 1.0, -1.0)
    chosen_rows = []
    for t in range(T):
        named = ids[t].astype(F32)
        hot = jnp.zeros((NR, R), F32)
        for k in range(4):
            hot = jnp.where(named[k : k + 1, :] == iota((NR, R), 0), 1.0, hot)
        code = (hot * (dot(hot.astype(BF16), earlier) + 1.0)).astype(BF16)
        place[t] = one_hot(dot(spread, dot(code, tile).astype(BF16)) == wants)
        code_t = dot_t(tile_t, code)
        mask_t[t] = jnp.where(dot(code_t.astype(BF16), spread_t) == wants_t, 1.0, 0.0)
        chosen_rows.append(jnp.where(code_t[:R] > 0, 1.0, 0.0))

    block_id = iota((1, 128), 1)
    own = jnp.zeros((1, 128), F32)
    taken = jnp.zeros((1, 128), F32)
    entry = iota((MIG * NB, 1), 0)
    entries = jnp.zeros((MIG * NB, 1), F32)
    for i in range(R * NB):
        named_block = table_s[i % NB, i // NB].astype(F32)
        if i < (R - MIG) * NB:
            own = jnp.where(block_id == named_block, 1.0, own)
        else:
            taken = jnp.where(block_id == named_block, 1.0, taken)
            entries = jnp.where(entry == i - (R - MIG) * NB, named_block, entries)
    below = one_hot(iota((128, 128), 0) < iota((128, 128), 1))
    marks = jnp.concatenate([1.0 - own, taken] + [jnp.zeros((1, 128), F32)] * 14, axis=0)
    ranks = dot(marks.astype(BF16), below)
    leaves = (ranks[0:1] == entry) & (own == 0)
    leaving = jnp.sum(jnp.where(leaves, block_id, 0.0), axis=1, keepdims=True)
    coming = jnp.sum(jnp.where(entries == block_id, ranks[1:2], 0.0), axis=1, keepdims=True)
    column = iota((MIG * NB, 128), 1)
    index_v[...] = jnp.where(column == 0, leaving, coming).astype(jnp.int32)
    to_smem = pltpu.make_async_copy(index_v, index_s, msem)
    to_smem.start()
    local[0].wait()
    for i in range((R - MIG) * NB):
        cache[i] = pool_v[table_s[i % NB, i // NB]]
    to_smem.wait()
    for i in range(MIG * NB):
        leave[i] = pool_v[jnp.clip(index_s[i, 0], 0, 127)]
    pl.semaphore_wait(barrier, len(greeted))

    def remote(src, dst, index, device):
        return pltpu.make_async_remote_copy(
            src_ref=src, dst_ref=dst, send_sem=ssend.at[index], recv_sem=srecv.at[index],
            device_id=device, device_id_type=MESH,
        )

    leave_copy = remote(leave, came, 1, {"replica": r_next})
    leave_copy.start()

    def gain_half(gain, h):
        return jnp.where(h == 0, gain[:, :H], gain[:, H:])

    def attn_half(t, h):
        x = xb[t, h].astype(F32) * gain_half(again, h)
        return dot(x.astype(BF16), wqkv_v[h])

    def attn_in(t):
        x = jnp.concatenate([xb[t, 0], xb[t, 1]], axis=1).astype(F32)
        scale = lax.rsqrt(jnp.mean(x * x, axis=-1, keepdims=True) + EPS)
        qkv = (qp[t] + attn_half(t, oc)) * scale
        cosine, sine = rope_c[t], rope_s[t]

        def turned(v):
            width = v.shape[1]
            low = mod(iota((R, width), 1), 64) < 32
            return jnp.where(low, pltpu.roll(v, width - 32, 1), pltpu.roll(v, 32, 1))

        q = qkv[:, :256]
        q = q * jnp.concatenate([cosine, cosine], 1) + turned(q) * jnp.concatenate([sine, sine], 1)
        kv = qkv[:, 256:]
        keys = iota((R, 128), 1) < 64
        kv = kv * jnp.where(keys, cosine, 1.0) + jnp.where(keys, turned(kv) * sine, 0.0)
        fresh[pl.ds(t * R, R)] = kv.astype(BF16)
        fresh_out[t] = kv.astype(BF16)
        q = jnp.concatenate([q] * 4, axis=0)
        head = div(iota((64, 256), 1), 64) == div(iota((64, 256), 0), 16)
        q4[t] = dot(jnp.where(head, q, 0.0).astype(BF16), fold[...]).astype(BF16)

    def attend(t):
        q = q4[t]
        past = cache[...].reshape(R * 128, 128)
        new = fresh[pl.ds(0, R * (t + 1))]
        score = dot_t(q, past)
        score = jnp.concatenate([score[g * R : g * R + R] + bias[...] for g in range(4)], axis=0)
        recent = dot_t(q, new)
        width = R * (t + 1)
        same = mod(iota((64, width), 1), 16) == mod(iota((64, width), 0), 16)
        recent = jnp.where(same, recent, NEG)
        group = div(iota((64, 1), 0), 16)
        sink = jnp.zeros((64, 1), F32)
        for g in range(4):
            sink = jnp.where(group == g, sinks[0, g], sink)
        peak = jnp.maximum(jnp.max(score, -1, keepdims=True), jnp.max(recent, -1, keepdims=True))
        peak = jnp.maximum(peak, sink)
        past_w = jnp.exp(score - peak)
        new_w = jnp.exp(recent - peak)
        total = jnp.sum(past_w, -1, keepdims=True) + jnp.sum(new_w, -1, keepdims=True)
        share = 1.0 / (total + jnp.exp(sink - peak))
        merged = dot((past_w * share).astype(BF16), past) + dot((new_w * share).astype(BF16), new)
        wide = dot(merged.astype(BF16), rep[...])
        head = div(iota((64, 256), 1), 64) == div(iota((64, 256), 0), 16)
        wide = jnp.where(head, wide, 0.0)
        wide = wide[:R] + wide[R : 2 * R] + wide[2 * R : 3 * R] + wide[3 * R :]
        wide = wide.astype(BF16)
        asend[t] = dot(wide, wout_v[oc]).astype(BF16)
        remote(asend.at[t], arecv.at[t], 10 + t, sib).start()
        apo[t] = dot(wide, wout_v[c])

    def pair_sum(t):
        remote(asend.at[t], arecv.at[t], 10 + t, sib).wait_recv()
        ar[t, zh] = (apo[t] + arecv[t].astype(F32)).astype(BF16)
        for peer in z_peers:
            remote(ar.at[t, zh], ar.at[t, zh], 13 + t, peer).start()

    def wait_blocks(ref, sem):
        pltpu.make_async_copy(ref, ref, sem).wait()

    def all_sum(t):
        wait_blocks(ar.at[t, pl.ds(0, NZ - 1)], srecv.at[13 + t])
        total = xb[t, c].astype(F32) + (
            ar[t, 0].astype(F32) + ar[t, 1].astype(F32) + (ar[t, 2].astype(F32) + ar[t, 3].astype(F32))
        )
        half = total.astype(BF16)
        h1[t, c] = half
        remote(h1.at[t, c], h1.at[t, c], 16 + t, sib).start()
        stack = jnp.concatenate([half[:, i * CW : i * CW + CW] for i in range(3)], axis=0)
        disp[t] = dot(place[t], stack).astype(BF16).reshape(NR, 16, CW)
        for peer, device in r_targets:
            remote(disp.at[t, peer], recv.at[t, c, r], 22 + t, device).start()
        recv[t, c, r] = disp[t, r]

        @pl.when(s < NS - 1)
        def _():
            remote(h1.at[t, c], hx.at[t], 19 + t, {"section": after}).start()

    def shares(t):
        remote(h1.at[t, c], h1.at[t, c], 16 + t, sib).wait_recv()
        x = jnp.concatenate([h1[t, 0], h1[t, 1]], axis=1).astype(F32)
        scale = lax.rsqrt(jnp.mean(x * x, axis=-1, keepdims=True) + EPS)
        normal = (x * scale * fgain[...]).astype(BF16)
        gates = chosen_rows[t] / (1.0 + jnp.exp(-dot_t(normal, router[...])))
        share = gates / jnp.sum(gates, -1, keepdims=True)
        share = jnp.concatenate([share] * 3, axis=0)
        high = share.astype(BF16)
        low = (share - high.astype(F32)).astype(BF16)
        comb[t, 0] = (dot(high, spread_t) * mask_t[t]).astype(BF16)
        comb[t, 1] = (dot(low, spread_t) * mask_t[t]).astype(BF16)

    def relay(t):
        wait_blocks(recv.at[t, 0, pl.ds(0, NR - 1)], srecv.at[22 + t])
        remote(recv.at[t, c], recv.at[t, c], 25 + t, sib).start()

    def expert(t):
        def half(h):
            rows = dot(sel[...], recv[t, h].reshape(256, CW))
            rows = jnp.concatenate([rows[i * 80 : i * 80 + 80] for i in range(3)], axis=1)
            square = jnp.sum(rows * rows, axis=-1, keepdims=True)
            return square, dot((rows * gain_half(fgain, h)).astype(BF16), wgu_v[h])

        square, both = half(c)
        remote(recv.at[t, c], recv.at[t, c], 25 + t, sib).wait_recv()
        square_o, both_o = half(oc)
        both = (both + both_o) * lax.rsqrt((square + square_o) * (1.0 / D) + EPS)
        gate, up = both[:, :256], both[:, 256:]
        hidden = (gate / (1.0 + jnp.exp(-gate)) * up).astype(BF16)
        ysend[t] = dot(hidden, wdown_v[oc]).astype(BF16)
        remote(ysend.at[t], yrecv.at[t], 28 + t, sib).start()
        yo[t] = dot(hidden, wdown_v[c])

    def give_back(t):
        remote(ysend.at[t], yrecv.at[t], 28 + t, sib).wait_recv()
        y = (yo[t] + yrecv[t].astype(F32)).astype(BF16)
        stack = jnp.concatenate([y[:, i * CW : i * CW + CW] for i in range(3)], axis=0)
        rsend[t] = dot(pack[...], stack).astype(BF16).reshape(NR, 16, CW)
        for peer, device in r_targets:
            remote(rsend.at[t, peer], rrecv.at[t, r], 31 + t, device).start()
        rrecv[t, r] = rsend[t, r]

    def combine(t):
        wait_blocks(rrecv.at[t, pl.ds(0, NR - 1)], srecv.at[31 + t])
        rows = rrecv[t].reshape(256, CW)
        got = dot(comb[t, 0], rows) + dot(comb[t, 1], rows)
        psend[t] = jnp.concatenate([got[i * R : i * R + R] for i in range(3)], axis=1).astype(BF16)

        @pl.when(s < NS - 1)
        def _():
            for k in (2, 1, 3, 0):
                peer = {"section": after, "expert": lax.rem(e + 2 * k, 2 * NZ)}
                remote(psend.at[t], xin.at[t, zh], 34 + t, peer).start()

        @pl.when(s == NS - 1)
        def _():
            for peer in z_peers:
                remote(psend.at[t], fin.at[t, zh], 43 + t, peer).start()
            fin[t, zh] = psend[t]

    def total_of(first, parts):
        a, b, c_, d = (parts[k].astype(F32) for k in range(NZ))
        return (first.astype(F32) + (a + b + (c_ + d))).astype(BF16)

    def sum_in(t):
        wait_blocks(xin.at[t], srecv.at[34 + t])
        remote(h1.at[t, c], hx.at[t], 19 + t, {"section": after}).wait_recv()
        xb[t, c] = total_of(hx[t], xin.at[t])
        remote(xb.at[t, c], xb.at[t, c], 37 + t, sib).start()
        qp[t] = attn_half(t, c)

    def lane_columns(t, of):
        x = jnp.concatenate([of[t, 0], of[t, 1]], axis=1).astype(F32)
        quarter = jnp.zeros((R, 384), F32)
        for k in range(NZ):
            quarter = jnp.where(zh == k, x[:, k * 384 : k * 384 + 384], quarter)
        return jnp.where(c == 0, quarter[:, :192], quarter[:, 192:])

    def send_result(t):
        own = lane_columns(t, xb)
        bsend[t] = jnp.concatenate([own, jnp.zeros((R, 64), F32)], axis=1).astype(BF16)
        remote(bsend.at[t], brecv.at[t], 40 + t, {"section": before}).start()

    for copy in local[1:5]:
        copy.wait()

    @pl.when(s == 0)
    def _():
        for t in range(T):
            token_copies[2 * t].wait()
            token_copies[2 * t + 1].wait()
            qp[t] = attn_half(t, c)
            attn_in(t)

    for copy in local[5:]:
        copy.wait()
    leave_copy.wait_recv()
    for i in range(MIG * NB):
        cache[(R - MIG) * NB + i] = came[jnp.clip(index_s[i, 1], 0, MIG * NB - 1)]

    def on_arrival(t):
        @pl.when(s > 0)
        def _():
            sum_in(t)

    def attention(t):
        @pl.when(s > 0)
        def _():
            remote(xb.at[t, c], xb.at[t, c], 37 + t, sib).wait_recv()
            attn_in(t)

        attend(t)

    def result(t):
        @pl.when(s > 0)
        def _():
            send_result(t)

    steps = {
        "I": on_arrival, "A": attention, "B": pair_sum, "C": all_sum, "D": shares,
        "E": relay, "F": expert, "G": give_back, "H": combine, "S": result,
    }
    for name, t in ORDER:
        steps[name](t)

    @pl.when(s == NS - 1)
    def _():
        for t in range(T):
            wait_blocks(fin.at[t, pl.ds(0, NZ - 1)], srecv.at[43 + t])
            xf[t, c] = total_of(h1[t, c], fin.at[t])
            remote(xf.at[t, c], xf.at[t, c], 46 + t, sib).start()
        for t in range(T):
            remote(xf.at[t, c], xf.at[t, c], 46 + t, sib).wait_recv()
            out[t] = lane_columns(t, xf).astype(BF16)

    @pl.when(s < NS - 1)
    def _():
        for t in range(T):
            remote(bsend.at[t], brecv.at[t], 40 + t, {"section": before}).wait_recv()
            out[t] = brecv[t][:, :192]

    leave_copy.wait_send()

    def left(t, pairs):
        for index, ref in pairs:
            wait_blocks(ref, ssend.at[index + t])

    for t in range(T):
        left(t, (
            (10, asend.at[t]),
            (13, ar.at[t, pl.ds(0, NZ - 1)]),
            (16, h1.at[t, c]),
            (22, disp.at[t, pl.ds(0, NR - 1)]),
            (25, recv.at[t, c]),
            (28, ysend.at[t]),
            (31, rsend.at[t, pl.ds(0, NR - 1)]),
        ))

    @pl.when(s > 0)
    def _():
        for t in range(T):
            left(t, ((37, xb.at[t, c]), (40, bsend.at[t])))

    @pl.when(s < NS - 1)
    def _():
        for t in range(T):
            left(t, ((19, h1.at[t, c]), (34, xin.at[t])))

    @pl.when(s == NS - 1)
    def _():
        for t in range(T):
            left(t, ((43, fin.at[t, pl.ds(0, NZ - 1)]), (46, xf.at[t, c])))


def local_part(
    tokens, attn_gain, w_query, w_keyval, sinks, w_out, ffn_gain, router, w_gate_up, w_down,
    kv_pool, block_table, lengths, expert_ids,
):
    vmem = pl.BlockSpec(memory_space=pltpu.VMEM)
    smem = pl.BlockSpec(memory_space=pltpu.SMEM)
    hbm = pl.BlockSpec(memory_space=pltpu.HBM)
    operands = [
        (tokens, hbm),
        (attn_gain, vmem),
        (w_query[0], hbm),
        (w_keyval.reshape(D, 128), hbm),
        (sinks, smem),
        (w_out[0], hbm),
        (ffn_gain, vmem),
        (router[0].T, vmem),
        (w_gate_up[0, 0], hbm),
        (w_down[0, 0], hbm),
        (kv_pool.reshape(128, 16, 128), hbm),
        (block_table.T, smem),
        (lengths, smem),
        (expert_ids[0].transpose(0, 2, 1), vmem),
    ]
    V = pltpu.VMEM
    scratch = [
        V((2, H, 384), BF16), V((2, 256, H), BF16), V((2, H, 512), BF16), V((2, 256, H), BF16),
        V((128, 16, 128), BF16), V((128, 16, 128), BF16), V((MIG * NB, 16, 128), BF16),
        V((MIG * NB, 16, 128), BF16),
        V((MIG * NB, 128), jnp.int32), pltpu.SMEM((MIG * NB, 128), jnp.int32),
        V((T, 2, R, H), BF16), V((T, 2, R, H), BF16), V((T, 64, 128), BF16), V((T * R, 128), BF16),
        V((T, R, 128), F32), V((T, R, 128), F32), V((R, R * 128), F32),
        V((256, 128), BF16), V((128, 256), BF16), V((240, 256), BF16), V((256, 240), BF16),
        V((T, 256, 48), BF16), V((T, 48, 256), F32), V((T, 2, 48, 256), BF16),
        V((T, R, H), F32), V((T, R, H), BF16), V((T, R, H), BF16), V((T, NZ, R, H), BF16),
        V((T, 2, R, H), BF16), V((T, R, H), BF16), V((T, NR, 16, CW), BF16),
        V((T, 2, NR, 16, CW), BF16), V((T, 80, H), F32), V((T, 80, H), BF16), V((T, 80, H), BF16),
        V((T, NR, 16, CW), BF16), V((T, NR, 16, CW), BF16), V((T, R, H), BF16),
        V((T, NZ, R, H), BF16), V((T, R, 256), BF16), V((T, R, 256), BF16),
        V((T, R, 384), F32), V((T, NZ, R, H), BF16),
        pltpu.SemaphoreType.DMA((13,)), pltpu.SemaphoreType.DMA((2 * T,)), pltpu.SemaphoreType.DMA,
        pltpu.SemaphoreType.DMA((49,)), pltpu.SemaphoreType.DMA((49,)),
    ]
    layer_out, fresh = pl.pallas_call(
        kernel,
        out_shape=(
            jax.ShapeDtypeStruct((T, R, 192), BF16),
            jax.ShapeDtypeStruct((T, R, 128), BF16),
        ),
        in_specs=[spec for _, spec in operands],
        out_specs=(vmem, vmem),
        scratch_shapes=scratch,
        compiler_params=pltpu.CompilerParams(
            collective_id=0, has_side_effects=True, vmem_limit_bytes=62 << 20
        ),
        name="layers",
    )(*[value for value, _ in operands])
    return layer_out[None], fresh.reshape(1, T, R, 1, 128)


def solution(mesh):
    return jax.shard_map(
        local_part,
        mesh=mesh,
        in_specs=(
            P(None, "replica", None),
            P("section", None),
            P("section", None, "expert"),
            P("section", None, "expert", None),
            P("section", "expert"),
            P("section", "expert", None),
            P("section", None),
            P("section", None, None),
            P("section", "replica", None, None, "expert"),
            P("section", "replica", "expert", None),
            P("section", "replica", None, "expert", None),
            P("replica", None),
            P("replica"),
            P("section", None, "replica", None),
        ),
        out_specs=(
            P("section", None, "replica", "expert"),
            P("section", None, "replica", "expert", None),
        ),
        check_vma=False,
    )
```

```python
import math

import jax
import jax.numpy as jnp
from jax import lax
from jax.experimental import pallas as pl
from jax.experimental.pallas import tpu as pltpu
from jax.sharding import PartitionSpec as P

MESH = pl.DeviceIdType.MESH
F32 = jnp.float32
BF16 = jnp.bfloat16
EPS = 1e-05
THETA = 150000.0
NEG = -1e30
T = 3
R = 16
D = 1536
H = 768
CW = 256
NR = 16
NZ = 4
SLOT = 5
MIG = 4
NB = 8
NS = 4

ORDER = (
    ("I", 0), ("A", 0), ("B", 0), ("I", 1), ("S", 0), ("A", 1), ("B", 1), ("I", 2),
    ("A", 2), ("C", 0), ("B", 2), ("C", 1), ("D", 0), ("E", 0), ("D", 1), ("S", 1),
    ("F", 0), ("C", 2), ("G", 0), ("E", 1), ("S", 2), ("D", 2), ("F", 1), ("G", 1),
    ("E", 2), ("H", 0), ("F", 2), ("G", 2), ("H", 1), ("H", 2),
)


def iota(shape, axis):
    return lax.broadcasted_iota(jnp.int32, shape, axis).astype(F32)


def div(value, by):
    return jnp.floor((value + 0.5) * (1.0 / by))


def mod(value, by):
    return value - by * div(value, by)


def dot(a, b):
    return jnp.dot(a, b, preferred_element_type=F32)


def dot_t(a, b):
    return lax.dot_general(a, b, (((1,), (1,)), ((), ())), preferred_element_type=F32)


def one_hot(cond):
    return jnp.where(cond, 1.0, 0.0).astype(BF16)


def kernel(
    tok, again, wq, wkv, sinks, wout, fgain, router, wgu, wdown, pool, table_s, lens, ids,
    out, fresh_out,
    wqkv_v, wout_v, wgu_v, wdown_v, pool_v, cache, leave, came, index_v, index_s,
    xb, xf, q4, fresh, rope_c, rope_s, bias,
    fold, rep, sel, pack, place, mask_t, comb,
    apo, asend, arecv, ar, h1, hx, disp, recv, yo, ysend, yrecv, rsend, rrecv, psend, xin, bsend, brecv, qp, fin,
    wsem, tsem, msem, ssend, srecv,
):
    s = lax.axis_index("section")
    r = lax.axis_index("replica")
    e = lax.axis_index("expert")
    c = lax.rem(e, 2)
    zh = lax.div(e, 2)
    oc = 1 - c
    sib = {"expert": e + 1 - 2 * c}
    after = lax.rem(s + 1, NS)
    before = lax.rem(s + NS - 1, NS)
    r_next = lax.rem(r + 1, NR)
    r_prev = lax.rem(r + NR - 1, NR)
    z_peers = [{"expert": lax.rem(e + 2 * k, 2 * NZ)} for k in (2, 1, 3)]
    r_peers = [lax.rem(r + k, NR) for k in range(1, NR)]

    low = lax.div(r, NR // NZ)

    def hops(start, end):
        way = lax.rem(end - start + NZ, NZ)
        half_way = lax.div(way, 2) * (1 - lax.rem(way, 2))
        return lax.rem(way + 1, NZ) - 1 - NZ * lax.rem(start, 2) * half_way

    def lane_at(z):
        return 2 * lax.rem(lax.div(z + NZ * NZ, NZ), NZ) + c

    here = NZ * zh + low
    lane_to = [lane_at(here + hops(low, lax.div(p, NR // NZ))) for p in r_peers]
    lane_from = [lane_at(here - hops(lax.div(p, NR // NZ), low)) for p in r_peers]
    r_targets = [(p, {"replica": p, "expert": lane}) for p, lane in zip(r_peers, lane_to)]

    token_copies = [
        pltpu.make_async_copy(tok.at[t, :, pl.ds(h * H, H)], xb.at[t, h], tsem.at[2 * t + h])
        for t in range(T)
        for h in range(2)
    ]

    @pl.when(s == 0)
    def _():
        for copy in token_copies:
            copy.start()

    local = [(pool, pool_v)]
    for h in range(2):
        rows = pl.ds(h * H, H)
        local.append((wq.at[rows], wqkv_v.at[h, :, pl.ds(0, 256)]))
        local.append((wkv.at[rows], wqkv_v.at[h, :, pl.ds(256, 128)]))
    for h in range(2):
        local.append((wout.at[:, pl.ds(h * H, H)], wout_v.at[h]))
    for h in range(2):
        for k in range(2):
            local.append((wgu.at[k, pl.ds(h * H, H)], wgu_v.at[h, :, pl.ds(k * 256, 256)]))
    for h in range(2):
        local.append((wdown.at[:, pl.ds(h * H, H)], wdown_v.at[h]))
    local = [pltpu.make_async_copy(a, b, wsem.at[i]) for i, (a, b) in enumerate(local)]
    for copy in local:
        copy.start()

    barrier = pltpu.get_barrier_semaphore()
    greeted = [sib, {"replica": r_prev}, *z_peers, *[{"replica": p, "expert": lane} for p, lane in zip(r_peers, lane_from)]]
    for k in range(NZ):
        lane = lax.rem(e + 2 * k, 2 * NZ)
        greeted += [{"section": after, "expert": lane}, {"section": before, "expert": lane}]
    for peer in greeted:
        pl.semaphore_signal(barrier, inc=1, device_id=peer, device_id_type=MESH)

    row16 = iota((R, 1), 0)
    length = jnp.zeros((R, 1), F32)
    for i in range(R):
        length = jnp.where(row16 == i, lens[i].astype(F32), length)
    lane = iota((1, 128), 1)
    freq = jnp.exp(mod(lane, 32) * (-2.0 / 64 * math.log(THETA)))
    sign = jnp.where(mod(lane, 64) < 32, -1.0, 1.0)
    for t in range(T):
        angle = (length + float(t)) * freq
        rope_c[t] = jnp.cos(angle)
        rope_s[t] = jnp.sin(angle) * sign
    inside = iota((R, R * 128), 1) - iota((R, R * 128), 0) * 128.0
    bias[...] = jnp.where((inside >= 0) & (inside < length), 0.0, NEG)
    a, b = iota((256, 128), 0), iota((256, 128), 1)
    fold[...] = jnp.where(mod(a, 64) == b, 0.125, 0.0).astype(BF16)
    a, b = iota((128, 256), 0), iota((128, 256), 1)
    rep[...] = one_hot(a - 64 == mod(b, 64))

    def packed_at(q):
        block = div(q, R * SLOT)
        rest = q - block * (R * SLOT)
        source = div(rest, SLOT)
        return source * 16 + block * SLOT + rest - source * SLOT

    sel[...] = one_hot(packed_at(iota((240, 1), 0)) == iota((240, 256), 1))
    pack[...] = one_hot(packed_at(iota((1, 240), 1)) == iota((256, 240), 0))
    spread = one_hot(div(iota((256, NR), 0), 16) == iota((256, NR), 1))
    spread_t = one_hot(div(iota((NR, 256), 1), 16) == iota((NR, 256), 0))
    tile = one_hot(mod(iota((R, 48), 1), 16) == iota((R, 48), 0))
    tile_t = one_hot(mod(iota((48, R), 0), 16) == iota((48, R), 1))
    earlier = one_hot(iota((R, R), 0) < iota((R, R), 1))
    at = mod(iota((256, 48), 0), 16)
    block = div(at, SLOT)
    wants = jnp.where(block == div(iota((256, 48), 1), 16), at - block * SLOT + 1.0, -1.0)
    at_t = mod(iota((48, 256), 1), 16)
    block_t = div(at_t, SLOT)
    wants_t = jnp.where(block_t == div(iota((48, 256), 0), 16), at_t - block_t * SLOT + 1.0, -1.0)
    chosen_rows = []
    for t in range(T):
        named = ids[t].astype(F32)
        hot = jnp.zeros((NR, R), F32)
        for k in range(4):
            hot = jnp.where(named[k : k + 1, :] == iota((NR, R), 0), 1.0, hot)
        code = (hot * (dot(hot.astype(BF16), earlier) + 1.0)).astype(BF16)
        place[t] = one_hot(dot(spread, dot(code, tile).astype(BF16)) == wants)
        code_t = dot_t(tile_t, code)
        mask_t[t] = jnp.where(dot(code_t.astype(BF16), spread_t) == wants_t, 1.0, 0.0)
        chosen_rows.append(jnp.where(code_t[:R] > 0, 1.0, 0.0))

    block_id = iota((1, 128), 1)
    own = jnp.zeros((1, 128), F32)
    taken = jnp.zeros((1, 128), F32)
    entry = iota((MIG * NB, 1), 0)
    entries = jnp.zeros((MIG * NB, 1), F32)
    for i in range(R * NB):
        named_block = table_s[i % NB, i // NB].astype(F32)
        if i < (R - MIG) * NB:
            own = jnp.where(block_id == named_block, 1.0, own)
        else:
            taken = jnp.where(block_id == named_block, 1.0, taken)
            entries = jnp.where(entry == i - (R - MIG) * NB, named_block, entries)
    below = one_hot(iota((128, 128), 0) < iota((128, 128), 1))
    marks = jnp.concatenate([1.0 - own, taken] + [jnp.zeros((1, 128), F32)] * 14, axis=0)
    ranks = dot(marks.astype(BF16), below)
    leaves = (ranks[0:1] == entry) & (own == 0)
    leaving = jnp.sum(jnp.where(leaves, block_id, 0.0), axis=1, keepdims=True)
    coming = jnp.sum(jnp.where(entries == block_id, ranks[1:2], 0.0), axis=1, keepdims=True)
    column = iota((MIG * NB, 128), 1)
    index_v[...] = jnp.where(column == 0, leaving, coming).astype(jnp.int32)
    to_smem = pltpu.make_async_copy(index_v, index_s, msem)
    to_smem.start()
    local[0].wait()
    for i in range((R - MIG) * NB):
        cache[i] = pool_v[table_s[i % NB, i // NB]]
    to_smem.wait()
    for i in range(MIG * NB):
        leave[i] = pool_v[jnp.clip(index_s[i, 0], 0, 127)]
    pl.semaphore_wait(barrier, len(greeted))

    def remote(src, dst, index, device):
        return pltpu.make_async_remote_copy(
            src_ref=src, dst_ref=dst, send_sem=ssend.at[index], recv_sem=srecv.at[index],
            device_id=device, device_id_type=MESH,
        )

    leave_copy = remote(leave, came, 1, {"replica": r_next})
    leave_copy.start()

    def gain_half(gain, h):
        return jnp.where(h == 0, gain[:, :H], gain[:, H:])

    def attn_half(t, h):
        x = xb[t, h].astype(F32) * gain_half(again, h)
        return dot(x.astype(BF16), wqkv_v[h])

    def attn_in(t):
        x = jnp.concatenate([xb[t, 0], xb[t, 1]], axis=1).astype(F32)
        scale = lax.rsqrt(jnp.mean(x * x, axis=-1, keepdims=True) + EPS)
        qkv = (qp[t] + attn_half(t, oc)) * scale
        cosine, sine = rope_c[t], rope_s[t]

        def turned(v):
            width = v.shape[1]
            low = mod(iota((R, width), 1), 64) < 32
            return jnp.where(low, pltpu.roll(v, width - 32, 1), pltpu.roll(v, 32, 1))

        q = qkv[:, :256]
        q = q * jnp.concatenate([cosine, cosine], 1) + turned(q) * jnp.concatenate([sine, sine], 1)
        kv = qkv[:, 256:]
        keys = iota((R, 128), 1) < 64
        kv = kv * jnp.where(keys, cosine, 1.0) + jnp.where(keys, turned(kv) * sine, 0.0)
        fresh[pl.ds(t * R, R)] = kv.astype(BF16)
        fresh_out[t] = kv.astype(BF16)
        q = jnp.concatenate([q] * 4, axis=0)
        head = div(iota((64, 256), 1), 64) == div(iota((64, 256), 0), 16)
        q4[t] = dot(jnp.where(head, q, 0.0).astype(BF16), fold[...]).astype(BF16)

    def attend(t):
        q = q4[t]
        past = cache[...].reshape(R * 128, 128)
        new = fresh[pl.ds(0, R * (t + 1))]
        score = dot_t(q, past)
        score = jnp.concatenate([score[g * R : g * R + R] + bias[...] for g in range(4)], axis=0)
        recent = dot_t(q, new)
        width = R * (t + 1)
        same = mod(iota((64, width), 1), 16) == mod(iota((64, width), 0), 16)
        recent = jnp.where(same, recent, NEG)
        group = div(iota((64, 1), 0), 16)
        sink = jnp.zeros((64, 1), F32)
        for g in range(4):
            sink = jnp.where(group == g, sinks[0, g], sink)
        peak = jnp.maximum(jnp.max(score, -1, keepdims=True), jnp.max(recent, -1, keepdims=True))
        peak = jnp.maximum(peak, sink)
        past_w = jnp.exp(score - peak)
        new_w = jnp.exp(recent - peak)
        total = jnp.sum(past_w, -1, keepdims=True) + jnp.sum(new_w, -1, keepdims=True)
        share = 1.0 / (total + jnp.exp(sink - peak))
        merged = dot((past_w * share).astype(BF16), past) + dot((new_w * share).astype(BF16), new)
        wide = dot(merged.astype(BF16), rep[...])
        head = div(iota((64, 256), 1), 64) == div(iota((64, 256), 0), 16)
        wide = jnp.where(head, wide, 0.0)
        wide = wide[:R] + wide[R : 2 * R] + wide[2 * R : 3 * R] + wide[3 * R :]
        wide = wide.astype(BF16)
        asend[t] = dot(wide, wout_v[oc]).astype(BF16)
        remote(asend.at[t], arecv.at[t], 10 + t, sib).start()
        apo[t] = dot(wide, wout_v[c])

    def pair_sum(t):
        remote(asend.at[t], arecv.at[t], 10 + t, sib).wait_recv()
        ar[t, zh] = (apo[t] + arecv[t].astype(F32)).astype(BF16)
        for peer in z_peers:
            remote(ar.at[t, zh], ar.at[t, zh], 13 + t, peer).start()

    def wait_blocks(ref, sem):
        pltpu.make_async_copy(ref, ref, sem).wait()

    def all_sum(t):
        wait_blocks(ar.at[t, pl.ds(0, NZ - 1)], srecv.at[13 + t])
        total = xb[t, c].astype(F32) + (
            ar[t, 0].astype(F32) + ar[t, 1].astype(F32) + (ar[t, 2].astype(F32) + ar[t, 3].astype(F32))
        )
        half = total.astype(BF16)
        h1[t, c] = half
        remote(h1.at[t, c], h1.at[t, c], 16 + t, sib).start()
        stack = jnp.concatenate([half[:, i * CW : i * CW + CW] for i in range(3)], axis=0)
        disp[t] = dot(place[t], stack).astype(BF16).reshape(NR, 16, CW)
        for peer, device in r_targets:
            remote(disp.at[t, peer], recv.at[t, c, r], 22 + t, device).start()
        recv[t, c, r] = disp[t, r]

        @pl.when(s < NS - 1)
        def _():
            remote(h1.at[t, c], hx.at[t], 19 + t, {"section": after}).start()

    def shares(t):
        remote(h1.at[t, c], h1.at[t, c], 16 + t, sib).wait_recv()
        x = jnp.concatenate([h1[t, 0], h1[t, 1]], axis=1).astype(F32)
        scale = lax.rsqrt(jnp.mean(x * x, axis=-1, keepdims=True) + EPS)
        normal = (x * scale * fgain[...]).astype(BF16)
        gates = chosen_rows[t] / (1.0 + jnp.exp(-dot_t(normal, router[...])))
        share = gates / jnp.sum(gates, -1, keepdims=True)
        share = jnp.concatenate([share] * 3, axis=0)
        high = share.astype(BF16)
        low = (share - high.astype(F32)).astype(BF16)
        comb[t, 0] = (dot(high, spread_t) * mask_t[t]).astype(BF16)
        comb[t, 1] = (dot(low, spread_t) * mask_t[t]).astype(BF16)

    def relay(t):
        wait_blocks(recv.at[t, 0, pl.ds(0, NR - 1)], srecv.at[22 + t])
        remote(recv.at[t, c], recv.at[t, c], 25 + t, sib).start()

    def expert(t):
        def half(h):
            rows = dot(sel[...], recv[t, h].reshape(256, CW))
            rows = jnp.concatenate([rows[i * 80 : i * 80 + 80] for i in range(3)], axis=1)
            square = jnp.sum(rows * rows, axis=-1, keepdims=True)
            return square, dot((rows * gain_half(fgain, h)).astype(BF16), wgu_v[h])

        square, both = half(c)
        remote(recv.at[t, c], recv.at[t, c], 25 + t, sib).wait_recv()
        square_o, both_o = half(oc)
        both = (both + both_o) * lax.rsqrt((square + square_o) * (1.0 / D) + EPS)
        gate, up = both[:, :256], both[:, 256:]
        hidden = (gate / (1.0 + jnp.exp(-gate)) * up).astype(BF16)
        ysend[t] = dot(hidden, wdown_v[oc]).astype(BF16)
        remote(ysend.at[t], yrecv.at[t], 28 + t, sib).start()
        yo[t] = dot(hidden, wdown_v[c])

    def give_back(t):
        remote(ysend.at[t], yrecv.at[t], 28 + t, sib).wait_recv()
        y = (yo[t] + yrecv[t].astype(F32)).astype(BF16)
        stack = jnp.concatenate([y[:, i * CW : i * CW + CW] for i in range(3)], axis=0)
        rsend[t] = dot(pack[...], stack).astype(BF16).reshape(NR, 16, CW)
        for peer, device in r_targets:
            remote(rsend.at[t, peer], rrecv.at[t, r], 31 + t, device).start()
        rrecv[t, r] = rsend[t, r]

    def combine(t):
        wait_blocks(rrecv.at[t, pl.ds(0, NR - 1)], srecv.at[31 + t])
        rows = rrecv[t].reshape(256, CW)
        got = dot(comb[t, 0], rows) + dot(comb[t, 1], rows)
        psend[t] = jnp.concatenate([got[i * R : i * R + R] for i in range(3)], axis=1).astype(BF16)

        @pl.when(s < NS - 1)
        def _():
            for k in (2, 1, 3, 0):
                peer = {"section": after, "expert": lax.rem(e + 2 * k, 2 * NZ)}
                remote(psend.at[t], xin.at[t, zh], 34 + t, peer).start()

        @pl.when(s == NS - 1)
        def _():
            for peer in z_peers:
                remote(psend.at[t], fin.at[t, zh], 43 + t, peer).start()
            fin[t, zh] = psend[t]

    def total_of(first, parts):
        a, b, c_, d = (parts[k].astype(F32) for k in range(NZ))
        return (first.astype(F32) + (a + b + (c_ + d))).astype(BF16)

    def sum_in(t):
        wait_blocks(xin.at[t], srecv.at[34 + t])
        remote(h1.at[t, c], hx.at[t], 19 + t, {"section": after}).wait_recv()
        xb[t, c] = total_of(hx[t], xin.at[t])
        remote(xb.at[t, c], xb.at[t, c], 37 + t, sib).start()
        qp[t] = attn_half(t, c)

    def lane_columns(t, of):
        x = jnp.concatenate([of[t, 0], of[t, 1]], axis=1).astype(F32)
        quarter = jnp.zeros((R, 384), F32)
        for k in range(NZ):
            quarter = jnp.where(zh == k, x[:, k * 384 : k * 384 + 384], quarter)
        return jnp.where(c == 0, quarter[:, :192], quarter[:, 192:])

    def send_result(t):
        own = lane_columns(t, xb)
        bsend[t] = jnp.concatenate([own, jnp.zeros((R, 64), F32)], axis=1).astype(BF16)
        remote(bsend.at[t], brecv.at[t], 40 + t, {"section": before}).start()

    for copy in local[1:5]:
        copy.wait()

    @pl.when(s == 0)
    def _():
        for t in range(T):
            token_copies[2 * t].wait()
            token_copies[2 * t + 1].wait()
            qp[t] = attn_half(t, c)
            attn_in(t)

    for copy in local[5:]:
        copy.wait()
    leave_copy.wait_recv()
    for i in range(MIG * NB):
        cache[(R - MIG) * NB + i] = came[jnp.clip(index_s[i, 1], 0, MIG * NB - 1)]

    def on_arrival(t):
        @pl.when(s > 0)
        def _():
            sum_in(t)

    def attention(t):
        @pl.when(s > 0)
        def _():
            remote(xb.at[t, c], xb.at[t, c], 37 + t, sib).wait_recv()
            attn_in(t)

        attend(t)

    def result(t):
        @pl.when(s > 0)
        def _():
            send_result(t)

    steps = {
        "I": on_arrival, "A": attention, "B": pair_sum, "C": all_sum, "D": shares,
        "E": relay, "F": expert, "G": give_back, "H": combine, "S": result,
    }
    for name, t in ORDER:
        steps[name](t)

    @pl.when(s == NS - 1)
    def _():
        for t in range(T):
            wait_blocks(fin.at[t, pl.ds(0, NZ - 1)], srecv.at[43 + t])
            xf[t, c] = total_of(h1[t, c], fin.at[t])
            remote(xf.at[t, c], xf.at[t, c], 46 + t, sib).start()
        for t in range(T):
            remote(xf.at[t, c], xf.at[t, c], 46 + t, sib).wait_recv()
            out[t] = lane_columns(t, xf).astype(BF16)

    @pl.when(s < NS - 1)
    def _():
        for t in range(T):
            remote(bsend.at[t], brecv.at[t], 40 + t, {"section": before}).wait_recv()
            out[t] = brecv[t][:, :192]

    leave_copy.wait_send()

    def left(t, pairs):
        for index, ref in pairs:
            wait_blocks(ref, ssend.at[index + t])

    for t in range(T):
        left(t, (
            (10, asend.at[t]),
            (13, ar.at[t, pl.ds(0, NZ - 1)]),
            (16, h1.at[t, c]),
            (22, disp.at[t, pl.ds(0, NR - 1)]),
            (25, recv.at[t, c]),
            (28, ysend.at[t]),
            (31, rsend.at[t, pl.ds(0, NR - 1)]),
        ))

    @pl.when(s > 0)
    def _():
        for t in range(T):
            left(t, ((37, xb.at[t, c]), (40, bsend.at[t])))

    @pl.when(s < NS - 1)
    def _():
        for t in range(T):
            left(t, ((19, h1.at[t, c]), (34, xin.at[t])))

    @pl.when(s == NS - 1)
    def _():
        for t in range(T):
            left(t, ((43, fin.at[t, pl.ds(0, NZ - 1)]), (46, xf.at[t, c])))


def local_part(
    tokens, attn_gain, w_query, w_keyval, sinks, w_out, ffn_gain, router, w_gate_up, w_down,
    kv_pool, block_table, lengths, expert_ids,
):
    vmem = pl.BlockSpec(memory_space=pltpu.VMEM)
    smem = pl.BlockSpec(memory_space=pltpu.SMEM)
    hbm = pl.BlockSpec(memory_space=pltpu.HBM)
    operands = [
        (tokens, hbm),
        (attn_gain, vmem),
        (w_query[0], hbm),
        (w_keyval.reshape(D, 128), hbm),
        (sinks, smem),
        (w_out[0], hbm),
        (ffn_gain, vmem),
        (router[0].T, vmem),
        (w_gate_up[0, 0], hbm),
        (w_down[0, 0], hbm),
        (kv_pool.reshape(128, 16, 128), hbm),
        (block_table.T, smem),
        (lengths, smem),
        (expert_ids[0].transpose(0, 2, 1), vmem),
    ]
    V = pltpu.VMEM
    scratch = [
        V((2, H, 384), BF16), V((2, 256, H), BF16), V((2, H, 512), BF16), V((2, 256, H), BF16),
        V((128, 16, 128), BF16), V((128, 16, 128), BF16), V((MIG * NB, 16, 128), BF16),
        V((MIG * NB, 16, 128), BF16),
        V((MIG * NB, 128), jnp.int32), pltpu.SMEM((MIG * NB, 128), jnp.int32),
        V((T, 2, R, H), BF16), V((T, 2, R, H), BF16), V((T, 64, 128), BF16), V((T * R, 128), BF16),
        V((T, R, 128), F32), V((T, R, 128), F32), V((R, R * 128), F32),
        V((256, 128), BF16), V((128, 256), BF16), V((240, 256), BF16), V((256, 240), BF16),
        V((T, 256, 48), BF16), V((T, 48, 256), F32), V((T, 2, 48, 256), BF16),
        V((T, R, H), F32), V((T, R, H), BF16), V((T, R, H), BF16), V((T, NZ, R, H), BF16),
        V((T, 2, R, H), BF16), V((T, R, H), BF16), V((T, NR, 16, CW), BF16),
        V((T, 2, NR, 16, CW), BF16), V((T, 80, H), F32), V((T, 80, H), BF16), V((T, 80, H), BF16),
        V((T, NR, 16, CW), BF16), V((T, NR, 16, CW), BF16), V((T, R, H), BF16),
        V((T, NZ, R, H), BF16), V((T, R, 256), BF16), V((T, R, 256), BF16),
        V((T, R, 384), F32), V((T, NZ, R, H), BF16),
        pltpu.SemaphoreType.DMA((13,)), pltpu.SemaphoreType.DMA((2 * T,)), pltpu.SemaphoreType.DMA,
        pltpu.SemaphoreType.DMA((49,)), pltpu.SemaphoreType.DMA((49,)),
    ]
    layer_out, fresh = pl.pallas_call(
        kernel,
        out_shape=(
            jax.ShapeDtypeStruct((T, R, 192), BF16),
            jax.ShapeDtypeStruct((T, R, 128), BF16),
        ),
        in_specs=[spec for _, spec in operands],
        out_specs=(vmem, vmem),
        scratch_shapes=scratch,
        compiler_params=pltpu.CompilerParams(
            collective_id=0, has_side_effects=True, vmem_limit_bytes=62 << 20
        ),
        name="layers",
    )(*[value for value, _ in operands])
    return layer_out[None], fresh.reshape(1, T, R, 1, 128)


def solution(mesh):
    return jax.shard_map(
        local_part,
        mesh=mesh,
        in_specs=(
            P(None, "replica", None),
            P("section", None),
            P("section", None, "expert"),
            P("section", None, "expert", None),
            P("section", "expert"),
            P("section", "expert", None),
            P("section", None),
            P("section", None, None),
            P("section", "replica", None, None, "expert"),
            P("section", "replica", "expert", None),
            P("section", "replica", None, "expert", None),
            P("replica", None),
            P("replica"),
            P("section", None, "replica", None),
        ),
        out_specs=(
            P("section", None, "replica", "expert"),
            P("section", None, "replica", "expert", None),
        ),
        check_vma=False,
    )
```

```python
import math

import jax
import jax.numpy as jnp
from jax import lax
from jax.experimental import pallas as pl
from jax.experimental.pallas import tpu as pltpu
from jax.sharding import PartitionSpec as P

MESH = pl.DeviceIdType.MESH
F32 = jnp.float32
BF16 = jnp.bfloat16
EPS = 1e-05
THETA = 150000.0
NEG = -1e30
T = 3
R = 16
D = 1536
H = 768
CW = 256
NR = 16
NZ = 4
SLOT = 5
MIG = 4
NB = 8
NS = 4

ORDER = (
    ("I", 0), ("A", 0), ("B", 0), ("I", 1), ("S", 0), ("A", 1), ("B", 1), ("I", 2),
    ("C", 0), ("A", 2), ("B", 2), ("C", 1), ("D", 0), ("E", 0), ("D", 1), ("S", 1),
    ("F", 0), ("C", 2), ("G", 0), ("E", 1), ("S", 2), ("D", 2), ("F", 1), ("G", 1),
    ("H", 0), ("E", 2), ("F", 2), ("G", 2), ("H", 1), ("H", 2),
)


def iota(shape, axis):
    return lax.broadcasted_iota(jnp.int32, shape, axis).astype(F32)


def div(value, by):
    return jnp.floor((value + 0.5) * (1.0 / by))


def mod(value, by):
    return value - by * div(value, by)


def dot(a, b):
    return jnp.dot(a, b, preferred_element_type=F32)


def dot_t(a, b):
    return lax.dot_general(a, b, (((1,), (1,)), ((), ())), preferred_element_type=F32)


def one_hot(cond):
    return jnp.where(cond, 1.0, 0.0).astype(BF16)


def kernel(
    tok, again, wq, wkv, sinks, wout, fgain, router, wgu, wdown, pool, table_s, lens, ids,
    out, fresh_out,
    wqkv_v, wout_v, wgu_v, wdown_v, pool_v, cache, leave, came, index_v, index_s,
    xb, xf, q4, fresh, rope_c, rope_s, bias,
    fold, rep, sel, pack, place, mask_t, comb,
    apo, asend, arecv, ar, h1, hx, disp, recv, yo, ysend, yrecv, rsend, rrecv, psend, xin, bsend, brecv, qp, fin,
    wsem, tsem, msem, ssend, srecv,
):
    s = lax.axis_index("section")
    r = lax.axis_index("replica")
    e = lax.axis_index("expert")
    c = lax.rem(e, 2)
    zh = lax.div(e, 2)
    oc = 1 - c
    sib = {"expert": e + 1 - 2 * c}
    after = lax.rem(s + 1, NS)
    before = lax.rem(s + NS - 1, NS)
    r_next = lax.rem(r + 1, NR)
    r_prev = lax.rem(r + NR - 1, NR)
    z_peers = [{"expert": lax.rem(e + 2 * k, 2 * NZ)} for k in (2, 1, 3)]
    r_peers = [lax.rem(r + k, NR) for k in range(1, NR)]

    low = lax.div(r, NR // NZ)

    def hops(start, end):
        way = lax.rem(end - start + NZ, NZ)
        half_way = lax.div(way, 2) * (1 - lax.rem(way, 2))
        return lax.rem(way + 1, NZ) - 1 - NZ * lax.rem(start, 2) * half_way

    def lane_at(z):
        return 2 * lax.rem(lax.div(z + NZ * NZ, NZ), NZ) + c

    here = NZ * zh + low
    lane_to = [lane_at(here + hops(low, lax.div(p, NR // NZ))) for p in r_peers]
    lane_from = [lane_at(here - hops(lax.div(p, NR // NZ), low)) for p in r_peers]
    r_targets = [(p, {"replica": p, "expert": lane}) for p, lane in zip(r_peers, lane_to)]

    token_copies = [
        pltpu.make_async_copy(tok.at[t, :, pl.ds(h * H, H)], xb.at[t, h], tsem.at[2 * t + h])
        for t in range(T)
        for h in range(2)
    ]

    @pl.when(s == 0)
    def _():
        for copy in token_copies:
            copy.start()

    local = [(pool, pool_v)]
    for h in range(2):
        rows = pl.ds(h * H, H)
        local.append((wq.at[rows], wqkv_v.at[h, :, pl.ds(0, 256)]))
        local.append((wkv.at[rows], wqkv_v.at[h, :, pl.ds(256, 128)]))
    for h in range(2):
        local.append((wout.at[:, pl.ds(h * H, H)], wout_v.at[h]))
    for h in range(2):
        for k in range(2):
            local.append((wgu.at[k, pl.ds(h * H, H)], wgu_v.at[h, :, pl.ds(k * 256, 256)]))
    for h in range(2):
        local.append((wdown.at[:, pl.ds(h * H, H)], wdown_v.at[h]))
    local = [pltpu.make_async_copy(a, b, wsem.at[i]) for i, (a, b) in enumerate(local)]
    for copy in local:
        copy.start()

    barrier = pltpu.get_barrier_semaphore()
    greeted = [sib, {"replica": r_prev}, *z_peers, *[{"replica": p, "expert": lane} for p, lane in zip(r_peers, lane_from)]]
    for k in range(NZ):
        lane = lax.rem(e + 2 * k, 2 * NZ)
        greeted += [{"section": after, "expert": lane}, {"section": before, "expert": lane}]
    for peer in greeted:
        pl.semaphore_signal(barrier, inc=1, device_id=peer, device_id_type=MESH)

    row16 = iota((R, 1), 0)
    length = jnp.zeros((R, 1), F32)
    for i in range(R):
        length = jnp.where(row16 == i, lens[i].astype(F32), length)
    lane = iota((1, 128), 1)
    freq = jnp.exp(mod(lane, 32) * (-2.0 / 64 * math.log(THETA)))
    sign = jnp.where(mod(lane, 64) < 32, -1.0, 1.0)
    for t in range(T):
        angle = (length + float(t)) * freq
        rope_c[t] = jnp.cos(angle)
        rope_s[t] = jnp.sin(angle) * sign
    inside = iota((R, R * 128), 1) - iota((R, R * 128), 0) * 128.0
    bias[...] = jnp.where((inside >= 0) & (inside < length), 0.0, NEG)
    a, b = iota((256, 128), 0), iota((256, 128), 1)
    fold[...] = jnp.where(mod(a, 64) == b, 0.125, 0.0).astype(BF16)
    a, b = iota((128, 256), 0), iota((128, 256), 1)
    rep[...] = one_hot(a - 64 == mod(b, 64))

    def packed_at(q):
        block = div(q, R * SLOT)
        rest = q - block * (R * SLOT)
        source = div(rest, SLOT)
        return source * 16 + block * SLOT + rest - source * SLOT

    sel[...] = one_hot(packed_at(iota((240, 1), 0)) == iota((240, 256), 1))
    pack[...] = one_hot(packed_at(iota((1, 240), 1)) == iota((256, 240), 0))
    spread = one_hot(div(iota((256, NR), 0), 16) == iota((256, NR), 1))
    spread_t = one_hot(div(iota((NR, 256), 1), 16) == iota((NR, 256), 0))
    tile = one_hot(mod(iota((R, 48), 1), 16) == iota((R, 48), 0))
    tile_t = one_hot(mod(iota((48, R), 0), 16) == iota((48, R), 1))
    earlier = one_hot(iota((R, R), 0) < iota((R, R), 1))
    at = mod(iota((256, 48), 0), 16)
    block = div(at, SLOT)
    wants = jnp.where(block == div(iota((256, 48), 1), 16), at - block * SLOT + 1.0, -1.0)
    at_t = mod(iota((48, 256), 1), 16)
    block_t = div(at_t, SLOT)
    wants_t = jnp.where(block_t == div(iota((48, 256), 0), 16), at_t - block_t * SLOT + 1.0, -1.0)
    chosen_rows = []
    for t in range(T):
        named = ids[t].astype(F32)
        hot = jnp.zeros((NR, R), F32)
        for k in range(4):
            hot = jnp.where(named[k : k + 1, :] == iota((NR, R), 0), 1.0, hot)
        code = (hot * (dot(hot.astype(BF16), earlier) + 1.0)).astype(BF16)
        place[t] = one_hot(dot(spread, dot(code, tile).astype(BF16)) == wants)
        code_t = dot_t(tile_t, code)
        mask_t[t] = jnp.where(dot(code_t.astype(BF16), spread_t) == wants_t, 1.0, 0.0)
        chosen_rows.append(jnp.where(code_t[:R] > 0, 1.0, 0.0))

    block_id = iota((1, 128), 1)
    own = jnp.zeros((1, 128), F32)
    taken = jnp.zeros((1, 128), F32)
    entry = iota((MIG * NB, 1), 0)
    entries = jnp.zeros((MIG * NB, 1), F32)
    for i in range(R * NB):
        named_block = table_s[i % NB, i // NB].astype(F32)
        if i < (R - MIG) * NB:
            own = jnp.where(block_id == named_block, 1.0, own)
        else:
            taken = jnp.where(block_id == named_block, 1.0, taken)
            entries = jnp.where(entry == i - (R - MIG) * NB, named_block, entries)
    below = one_hot(iota((128, 128), 0) < iota((128, 128), 1))
    marks = jnp.concatenate([1.0 - own, taken] + [jnp.zeros((1, 128), F32)] * 14, axis=0)
    ranks = dot(marks.astype(BF16), below)
    leaves = (ranks[0:1] == entry) & (own == 0)
    leaving = jnp.sum(jnp.where(leaves, block_id, 0.0), axis=1, keepdims=True)
    coming = jnp.sum(jnp.where(entries == block_id, ranks[1:2], 0.0), axis=1, keepdims=True)
    column = iota((MIG * NB, 128), 1)
    index_v[...] = jnp.where(column == 0, leaving, coming).astype(jnp.int32)
    to_smem = pltpu.make_async_copy(index_v, index_s, msem)
    to_smem.start()
    local[0].wait()
    for i in range((R - MIG) * NB):
        cache[i] = pool_v[table_s[i % NB, i // NB]]
    to_smem.wait()
    for i in range(MIG * NB):
        leave[i] = pool_v[jnp.clip(index_s[i, 0], 0, 127)]
    pl.semaphore_wait(barrier, len(greeted))

    def remote(src, dst, index, device):
        return pltpu.make_async_remote_copy(
            src_ref=src, dst_ref=dst, send_sem=ssend.at[index], recv_sem=srecv.at[index],
            device_id=device, device_id_type=MESH,
        )

    leave_copy = remote(leave, came, 1, {"replica": r_next})
    leave_copy.start()

    def gain_half(gain, h):
        return jnp.where(h == 0, gain[:, :H], gain[:, H:])

    def attn_half(t, h):
        x = xb[t, h].astype(F32) * gain_half(again, h)
        return dot(x.astype(BF16), wqkv_v[h])

    def attn_in(t):
        x = jnp.concatenate([xb[t, 0], xb[t, 1]], axis=1).astype(F32)
        scale = lax.rsqrt(jnp.mean(x * x, axis=-1, keepdims=True) + EPS)
        qkv = (qp[t] + attn_half(t, oc)) * scale
        cosine, sine = rope_c[t], rope_s[t]

        def turned(v):
            width = v.shape[1]
            low = mod(iota((R, width), 1), 64) < 32
            return jnp.where(low, pltpu.roll(v, width - 32, 1), pltpu.roll(v, 32, 1))

        q = qkv[:, :256]
        q = q * jnp.concatenate([cosine, cosine], 1) + turned(q) * jnp.concatenate([sine, sine], 1)
        kv = qkv[:, 256:]
        keys = iota((R, 128), 1) < 64
        kv = kv * jnp.where(keys, cosine, 1.0) + jnp.where(keys, turned(kv) * sine, 0.0)
        fresh[pl.ds(t * R, R)] = kv.astype(BF16)
        fresh_out[t] = kv.astype(BF16)
        q = jnp.concatenate([q] * 4, axis=0)
        head = div(iota((64, 256), 1), 64) == div(iota((64, 256), 0), 16)
        q4[t] = dot(jnp.where(head, q, 0.0).astype(BF16), fold[...]).astype(BF16)

    def attend(t):
        q = q4[t]
        past = cache[...].reshape(R * 128, 128)
        new = fresh[pl.ds(0, R * (t + 1))]
        score = dot_t(q, past)
        score = jnp.concatenate([score[g * R : g * R + R] + bias[...] for g in range(4)], axis=0)
        recent = dot_t(q, new)
        width = R * (t + 1)
        same = mod(iota((64, width), 1), 16) == mod(iota((64, width), 0), 16)
        recent = jnp.where(same, recent, NEG)
        group = div(iota((64, 1), 0), 16)
        sink = jnp.zeros((64, 1), F32)
        for g in range(4):
            sink = jnp.where(group == g, sinks[0, g], sink)
        peak = jnp.maximum(jnp.max(score, -1, keepdims=True), jnp.max(recent, -1, keepdims=True))
        peak = jnp.maximum(peak, sink)
        past_w = jnp.exp(score - peak)
        new_w = jnp.exp(recent - peak)
        total = jnp.sum(past_w, -1, keepdims=True) + jnp.sum(new_w, -1, keepdims=True)
        share = 1.0 / (total + jnp.exp(sink - peak))
        merged = dot((past_w * share).astype(BF16), past) + dot((new_w * share).astype(BF16), new)
        wide = dot(merged.astype(BF16), rep[...])
        head = div(iota((64, 256), 1), 64) == div(iota((64, 256), 0), 16)
        wide = jnp.where(head, wide, 0.0)
        wide = wide[:R] + wide[R : 2 * R] + wide[2 * R : 3 * R] + wide[3 * R :]
        wide = wide.astype(BF16)
        asend[t] = dot(wide, wout_v[oc]).astype(BF16)
        remote(asend.at[t], arecv.at[t], 10 + t, sib).start()
        apo[t] = dot(wide, wout_v[c])

    def pair_sum(t):
        remote(asend.at[t], arecv.at[t], 10 + t, sib).wait_recv()
        ar[t, zh] = (apo[t] + arecv[t].astype(F32)).astype(BF16)
        for peer in z_peers:
            remote(ar.at[t, zh], ar.at[t, zh], 13 + t, peer).start()

    def wait_blocks(ref, sem):
        pltpu.make_async_copy(ref, ref, sem).wait()

    def all_sum(t):
        wait_blocks(ar.at[t, pl.ds(0, NZ - 1)], srecv.at[13 + t])
        total = xb[t, c].astype(F32) + (
            ar[t, 0].astype(F32) + ar[t, 1].astype(F32) + (ar[t, 2].astype(F32) + ar[t, 3].astype(F32))
        )
        half = total.astype(BF16)
        h1[t, c] = half
        remote(h1.at[t, c], h1.at[t, c], 16 + t, sib).start()
        stack = jnp.concatenate([half[:, i * CW : i * CW + CW] for i in range(3)], axis=0)
        disp[t] = dot(place[t], stack).astype(BF16).reshape(NR, 16, CW)
        for peer, device in r_targets:
            remote(disp.at[t, peer], recv.at[t, c, r], 22 + t, device).start()
        recv[t, c, r] = disp[t, r]

        @pl.when(s < NS - 1)
        def _():
            remote(h1.at[t, c], hx.at[t], 19 + t, {"section": after}).start()

    def shares(t):
        remote(h1.at[t, c], h1.at[t, c], 16 + t, sib).wait_recv()
        x = jnp.concatenate([h1[t, 0], h1[t, 1]], axis=1).astype(F32)
        scale = lax.rsqrt(jnp.mean(x * x, axis=-1, keepdims=True) + EPS)
        normal = (x * scale * fgain[...]).astype(BF16)
        gates = chosen_rows[t] / (1.0 + jnp.exp(-dot_t(normal, router[...])))
        share = gates / jnp.sum(gates, -1, keepdims=True)
        share = jnp.concatenate([share] * 3, axis=0)
        high = share.astype(BF16)
        low = (share - high.astype(F32)).astype(BF16)
        comb[t, 0] = (dot(high, spread_t) * mask_t[t]).astype(BF16)
        comb[t, 1] = (dot(low, spread_t) * mask_t[t]).astype(BF16)

    def relay(t):
        wait_blocks(recv.at[t, 0, pl.ds(0, NR - 1)], srecv.at[22 + t])
        remote(recv.at[t, c], recv.at[t, c], 25 + t, sib).start()

    def expert(t):
        def half(h):
            rows = dot(sel[...], recv[t, h].reshape(256, CW))
            rows = jnp.concatenate([rows[i * 80 : i * 80 + 80] for i in range(3)], axis=1)
            square = jnp.sum(rows * rows, axis=-1, keepdims=True)
            return square, dot((rows * gain_half(fgain, h)).astype(BF16), wgu_v[h])

        square, both = half(c)
        remote(recv.at[t, c], recv.at[t, c], 25 + t, sib).wait_recv()
        square_o, both_o = half(oc)
        both = (both + both_o) * lax.rsqrt((square + square_o) * (1.0 / D) + EPS)
        gate, up = both[:, :256], both[:, 256:]
        hidden = (gate / (1.0 + jnp.exp(-gate)) * up).astype(BF16)
        ysend[t] = dot(hidden, wdown_v[oc]).astype(BF16)
        remote(ysend.at[t], yrecv.at[t], 28 + t, sib).start()
        yo[t] = dot(hidden, wdown_v[c])

    def give_back(t):
        remote(ysend.at[t], yrecv.at[t], 28 + t, sib).wait_recv()
        y = (yo[t] + yrecv[t].astype(F32)).astype(BF16)
        stack = jnp.concatenate([y[:, i * CW : i * CW + CW] for i in range(3)], axis=0)
        rsend[t] = dot(pack[...], stack).astype(BF16).reshape(NR, 16, CW)
        for peer, device in r_targets:
            remote(rsend.at[t, peer], rrecv.at[t, r], 31 + t, device).start()
        rrecv[t, r] = rsend[t, r]

    def combine(t):
        wait_blocks(rrecv.at[t, pl.ds(0, NR - 1)], srecv.at[31 + t])
        rows = rrecv[t].reshape(256, CW)
        got = dot(comb[t, 0], rows) + dot(comb[t, 1], rows)
        psend[t] = jnp.concatenate([got[i * R : i * R + R] for i in range(3)], axis=1).astype(BF16)

        @pl.when(s < NS - 1)
        def _():
            for k in (2, 1, 3, 0):
                peer = {"section": after, "expert": lax.rem(e + 2 * k, 2 * NZ)}
                remote(psend.at[t], xin.at[t, zh], 34 + t, peer).start()

        @pl.when(s == NS - 1)
        def _():
            for peer in z_peers:
                remote(psend.at[t], fin.at[t, zh], 43 + t, peer).start()
            fin[t, zh] = psend[t]

    def total_of(first, parts):
        a, b, c_, d = (parts[k].astype(F32) for k in range(NZ))
        return (first.astype(F32) + (a + b + (c_ + d))).astype(BF16)

    def sum_in(t):
        wait_blocks(xin.at[t], srecv.at[34 + t])
        remote(h1.at[t, c], hx.at[t], 19 + t, {"section": after}).wait_recv()
        xb[t, c] = total_of(hx[t], xin.at[t])
        remote(xb.at[t, c], xb.at[t, c], 37 + t, sib).start()
        qp[t] = attn_half(t, c)

    def lane_columns(t, of):
        x = jnp.concatenate([of[t, 0], of[t, 1]], axis=1).astype(F32)
        quarter = jnp.zeros((R, 384), F32)
        for k in range(NZ):
            quarter = jnp.where(zh == k, x[:, k * 384 : k * 384 + 384], quarter)
        return jnp.where(c == 0, quarter[:, :192], quarter[:, 192:])

    def send_result(t):
        own = lane_columns(t, xb)
        bsend[t] = jnp.concatenate([own, jnp.zeros((R, 64), F32)], axis=1).astype(BF16)
        remote(bsend.at[t], brecv.at[t], 40 + t, {"section": before}).start()

    for copy in local[1:5]:
        copy.wait()

    @pl.when(s == 0)
    def _():
        for t in range(T):
            token_copies[2 * t].wait()
            token_copies[2 * t + 1].wait()
            qp[t] = attn_half(t, c)
            attn_in(t)

    for copy in local[5:]:
        copy.wait()
    leave_copy.wait_recv()
    for i in range(MIG * NB):
        cache[(R - MIG) * NB + i] = came[jnp.clip(index_s[i, 1], 0, MIG * NB - 1)]

    def on_arrival(t):
        @pl.when(s > 0)
        def _():
            sum_in(t)

    def attention(t):
        @pl.when(s > 0)
        def _():
            remote(xb.at[t, c], xb.at[t, c], 37 + t, sib).wait_recv()
            attn_in(t)

        attend(t)

    def result(t):
        @pl.when(s > 0)
        def _():
            send_result(t)

    steps = {
        "I": on_arrival, "A": attention, "B": pair_sum, "C": all_sum, "D": shares,
        "E": relay, "F": expert, "G": give_back, "H": combine, "S": result,
    }
    for name, t in ORDER:
        steps[name](t)

    @pl.when(s == NS - 1)
    def _():
        for t in range(T):
            wait_blocks(fin.at[t, pl.ds(0, NZ - 1)], srecv.at[43 + t])
            xf[t, c] = total_of(h1[t, c], fin.at[t])
            remote(xf.at[t, c], xf.at[t, c], 46 + t, sib).start()
        for t in range(T):
            remote(xf.at[t, c], xf.at[t, c], 46 + t, sib).wait_recv()
            out[t] = lane_columns(t, xf).astype(BF16)

    @pl.when(s < NS - 1)
    def _():
        for t in range(T):
            remote(bsend.at[t], brecv.at[t], 40 + t, {"section": before}).wait_recv()
            out[t] = brecv[t][:, :192]

    leave_copy.wait_send()

    def left(t, pairs):
        for index, ref in pairs:
            wait_blocks(ref, ssend.at[index + t])

    for t in range(T):
        left(t, (
            (10, asend.at[t]),
            (13, ar.at[t, pl.ds(0, NZ - 1)]),
            (16, h1.at[t, c]),
            (22, disp.at[t, pl.ds(0, NR - 1)]),
            (25, recv.at[t, c]),
            (28, ysend.at[t]),
            (31, rsend.at[t, pl.ds(0, NR - 1)]),
        ))

    @pl.when(s > 0)
    def _():
        for t in range(T):
            left(t, ((37, xb.at[t, c]), (40, bsend.at[t])))

    @pl.when(s < NS - 1)
    def _():
        for t in range(T):
            left(t, ((19, h1.at[t, c]), (34, xin.at[t])))

    @pl.when(s == NS - 1)
    def _():
        for t in range(T):
            left(t, ((43, fin.at[t, pl.ds(0, NZ - 1)]), (46, xf.at[t, c])))


def local_part(
    tokens, attn_gain, w_query, w_keyval, sinks, w_out, ffn_gain, router, w_gate_up, w_down,
    kv_pool, block_table, lengths, expert_ids,
):
    vmem = pl.BlockSpec(memory_space=pltpu.VMEM)
    smem = pl.BlockSpec(memory_space=pltpu.SMEM)
    hbm = pl.BlockSpec(memory_space=pltpu.HBM)
    operands = [
        (tokens, hbm),
        (attn_gain, vmem),
        (w_query[0], hbm),
        (w_keyval.reshape(D, 128), hbm),
        (sinks, smem),
        (w_out[0], hbm),
        (ffn_gain, vmem),
        (router[0].T, vmem),
        (w_gate_up[0, 0], hbm),
        (w_down[0, 0], hbm),
        (kv_pool.reshape(128, 16, 128), hbm),
        (block_table.T, smem),
        (lengths, smem),
        (expert_ids[0].transpose(0, 2, 1), vmem),
    ]
    V = pltpu.VMEM
    scratch = [
        V((2, H, 384), BF16), V((2, 256, H), BF16), V((2, H, 512), BF16), V((2, 256, H), BF16),
        V((128, 16, 128), BF16), V((128, 16, 128), BF16), V((MIG * NB, 16, 128), BF16),
        V((MIG * NB, 16, 128), BF16),
        V((MIG * NB, 128), jnp.int32), pltpu.SMEM((MIG * NB, 128), jnp.int32),
        V((T, 2, R, H), BF16), V((T, 2, R, H), BF16), V((T, 64, 128), BF16), V((T * R, 128), BF16),
        V((T, R, 128), F32), V((T, R, 128), F32), V((R, R * 128), F32),
        V((256, 128), BF16), V((128, 256), BF16), V((240, 256), BF16), V((256, 240), BF16),
        V((T, 256, 48), BF16), V((T, 48, 256), F32), V((T, 2, 48, 256), BF16),
        V((T, R, H), F32), V((T, R, H), BF16), V((T, R, H), BF16), V((T, NZ, R, H), BF16),
        V((T, 2, R, H), BF16), V((T, R, H), BF16), V((T, NR, 16, CW), BF16),
        V((T, 2, NR, 16, CW), BF16), V((T, 80, H), F32), V((T, 80, H), BF16), V((T, 80, H), BF16),
        V((T, NR, 16, CW), BF16), V((T, NR, 16, CW), BF16), V((T, R, H), BF16),
        V((T, NZ, R, H), BF16), V((T, R, 256), BF16), V((T, R, 256), BF16),
        V((T, R, 384), F32), V((T, NZ, R, H), BF16),
        pltpu.SemaphoreType.DMA((13,)), pltpu.SemaphoreType.DMA((2 * T,)), pltpu.SemaphoreType.DMA,
        pltpu.SemaphoreType.DMA((49,)), pltpu.SemaphoreType.DMA((49,)),
    ]
    layer_out, fresh = pl.pallas_call(
        kernel,
        out_shape=(
            jax.ShapeDtypeStruct((T, R, 192), BF16),
            jax.ShapeDtypeStruct((T, R, 128), BF16),
        ),
        in_specs=[spec for _, spec in operands],
        out_specs=(vmem, vmem),
        scratch_shapes=scratch,
        compiler_params=pltpu.CompilerParams(
            collective_id=0, has_side_effects=True, vmem_limit_bytes=62 << 20
        ),
        name="layers",
    )(*[value for value, _ in operands])
    return layer_out[None], fresh.reshape(1, T, R, 1, 128)


def solution(mesh):
    return jax.shard_map(
        local_part,
        mesh=mesh,
        in_specs=(
            P(None, "replica", None),
            P("section", None),
            P("section", None, "expert"),
            P("section", None, "expert", None),
            P("section", "expert"),
            P("section", "expert", None),
            P("section", None),
            P("section", None, None),
            P("section", "replica", None, None, "expert"),
            P("section", "replica", "expert", None),
            P("section", "replica", None, "expert", None),
            P("replica", None),
            P("replica"),
            P("section", None, "replica", None),
        ),
        out_specs=(
            P("section", None, "replica", "expert"),
            P("section", None, "replica", "expert", None),
        ),
        check_vma=False,
    )
```
